32 devices in a mesh: group: 2 (over x), cell: 16 (over z, y, core).
Axes of the slice: x: 2, y: 2, z: 4, core: 2. Of those that a mesh axis runs over, the one named last changes fastest.
Arguments:
- adjoint_seed: float32 [32, 5, 16384], P('group', None, 'cell'), parts along dimension 0, may hold values from -6 to 6
- inv_blocks: bfloat16 [32, 5, 5, 16384], P('group', None, None, 'cell'), parts along dimension 0
- flux_jacobians: float32 [2, 32, 5, 5], P(None, 'group'), parts along dimension 1, may hold values from -1.5 to 1.5
- modal_shapes: float32 [20, 5, 16384], P(None, None, 'cell'), may hold values from -0.01953125 to 0.01953125
- modal_gain: float32 [40], P('group'), parts along dimension 0, may hold values from 0.05 to 0.3
- face_cells: int32 [2, 49152], P(None, 'cell'), may hold values from 0 to 1279, as said below
- face_weights: float32 [49152], P('cell'), may hold values from 0.4 to 1
- colours: int32 [16384], P('cell'), may hold values from 0 to 1
- send_cells: int32 [2, 2048], P(None, 'cell'), may hold values from 0 to 1023, as said below
Outputs:
- adjoint_state: float32 [32, 5, 16384], P('group', None, 'cell'), parts along dimension 0
- modal_partials: float32 [32, 20], P('group'), parts along dimension 0
The draws below stay inside these ranges and needn't reach their ends.
There are 2 independent parts, one for each index of `group`. The reference program is written for one: setup_inputs(seed, part) draws one part's arguments, and reference() takes and returns one part's arrays. A program takes and returns all parts, laid end to end along the dimension named above; an argument that names none is the same for every part. Nothing has to cross between parts.
Inputs may be any that keep to these rules, and one draw needn't show every extreme that they name: `face_cells`: each face's left cell is a local cell or a lower ghost (from 1024 to 1151); its right cell is a local cell or an upper ghost (from 1152 on). `send_cells`: within a partition the 256 listed cells are distinct local cells.
All inputs are finite; a program needn't handle non-finite values.
Results may differ from the reference program's by a relative error of at most 0.0003.
Values sent between devices are 32-bit elements; how exact they have to be, the bound alone decides.
A program may use at most 64 MiB of HBM per device.

```python
import math
import jax
import jax.numpy as jnp
from jax import lax

NI = 16
NV = 5
MODES = 20
ITERS = 4
CELLS_DEV = 1024
HALO = 128
FACES_DEV = 3072
CELLS = 16384
FACES = 49152
HALOS = 2048
N_CELL = 16


def draw_inv_blocks(key, part):
    first, second = jax.random.split(jax.random.fold_in(key, 11))
    diagonal = jnp.exp(jax.random.uniform(first, (NI, NV, CELLS), jnp.float32, jnp.log(0.25), jnp.log(0.6)))
    offdiag = 0.1 * jax.random.normal(second, (NI, NV, NV, CELLS), jnp.float32)
    unit = jnp.eye(NV, dtype=jnp.float32)[None, :, :, None]
    blocks = offdiag * (1.0 - unit) + diagonal[:, :, None, :] * unit
    return blocks.astype(jnp.bfloat16)


def draw_face_cells(key, part):
    count = FACES // FACES_DEV
    keys = jax.random.split(jax.random.fold_in(key, 23), 4)
    owner = jax.random.randint(keys[0], (count, FACES_DEV), 0, CELLS_DEV)
    step = jax.random.randint(keys[1], (count, FACES_DEV), 1, 3 * HALO)
    reach = owner + step
    right_cells = jnp.where(reach < CELLS_DEV, reach, CELLS_DEV + HALO + (reach - CELLS_DEV) % HALO)
    lowered = jax.random.randint(keys[2], (count, FACES_DEV), 0, 8) == 0
    left_cells = jnp.where(lowered, CELLS_DEV + jax.random.randint(keys[3], (count, FACES_DEV), 0, HALO), owner)
    return jnp.stack([left_cells, right_cells]).reshape(2, FACES).astype(jnp.int32)


def draw_send_cells(key, part):
    count = HALOS // HALO
    keys = jax.random.split(jax.random.fold_in(key, 37), count)
    chosen = jax.vmap(lambda single: jax.random.permutation(single, CELLS_DEV)[:2 * HALO])(keys)
    chosen = chosen.reshape(count, 2, HALO)
    return jnp.transpose(chosen, (1, 0, 2)).reshape(2, HALOS).astype(jnp.int32)


def with_ends(drawn, stream_key, low, largest):
    longest = drawn.shape.index(max(drawn.shape))
    spots = []
    for shift in (0, 1):
        where = [jax.random.randint(jax.random.fold_in(stream_key, axis), (), 0, length) for axis, length in enumerate(drawn.shape)]
        where[longest] = (where[longest] + shift) % drawn.shape[longest]
        spots.append(tuple(where))
    return drawn.at[spots[0]].set(low).at[spots[1]].set(largest)


def block_scale(key, extent, shards, low, largest):
    loudness, own = 1.0, jax.random.fold_in(key, 6)
    for dim, blocks in shards:
        steps = jnp.exp(jax.random.uniform(jax.random.fold_in(own, dim), (blocks,), jnp.float32, low / len(shards), largest / len(shards)))
        loudness = loudness * jnp.repeat(steps, extent[dim] // blocks).reshape([-1 if axis == dim else 1 for axis in range(len(extent))])
    return loudness


def gaussian(stream_key, shape, scale, bound, pieces=(), kind=jnp.bfloat16):
    values = jax.random.normal(stream_key, shape, jnp.float32) * scale
    if len(pieces) > 0:
        values = block_scale(stream_key, shape, pieces, -0.22, 0.18) * values
    return jnp.clip(values, min=-bound, max=bound).astype(kind)


def setup_inputs(seed: int = 0, part: int = 0) -> dict:
    key_list = jax.random.split(jax.random.key(seed), 10)
    part_keys = jax.random.split(jax.random.fold_in(key_list[9], part), 10)
    return {
        "adjoint_seed": gaussian(part_keys[0], (NI, NV, CELLS), 1.0, 6.0, ((2, 16),), jnp.float32),
        "inv_blocks": draw_inv_blocks(jax.random.fold_in(jax.random.fold_in(key_list[9], part), 71), part),
        "flux_jacobians": gaussian(part_keys[2], (2, NI, NV, NV), 0.25, 1.5, (), jnp.float32),
        "modal_shapes": gaussian(key_list[3], (MODES, NV, CELLS), (NV * CELLS) ** -0.5, 0.01953125, ((2, 16),), jnp.float32),
        "modal_gain": jnp.clip(jnp.exp(jax.random.uniform(part_keys[4], (MODES,), jnp.float32, math.log(0.05), math.log(0.3))), 0.05, 0.3),
        "face_cells": draw_face_cells(jax.random.fold_in(key_list[9], 71), part),
        "face_weights": jnp.clip(0.4 + 0.6 * jax.random.uniform(key_list[6], (FACES,), jnp.float32) ** block_scale(key_list[6], (FACES,), ((0, 16),), -0.2, 0.2), 0.4, 1.0),
        "colours": with_ends(jax.random.randint(key_list[7], (CELLS,), 0, 2), jax.random.fold_in(key_list[7], 1), 0, 1).astype(jnp.int32),
        "send_cells": draw_send_cells(jax.random.fold_in(key_list[9], 71), part),
    }


frequency = 0.04


def spectral_matrix(count):
    index = jnp.arange(count)
    apart = index[:, None] - index[None, :]
    angle = math.pi * apart.astype(jnp.float32) / count
    parity = jnp.where(apart % 2 == 0, 1.0, -1.0).astype(jnp.float32)
    safe_sin = jnp.where(apart == 0, 1.0, jnp.sin(angle))
    return jnp.where(apart == 0, 0.0, 0.5 * parity * jnp.cos(angle) / safe_sin).astype(jnp.float32)


def off_product(extended, jacobians, faces, weights, owned):
    left_cells = faces[0]
    right_cells = faces[1]
    from_left = jnp.einsum('nvw,nvc->nwc', jacobians[0], extended, precision=lax.Precision.HIGHEST)
    from_right = jnp.einsum('nvw,nvc->nwc', jacobians[1], extended, precision=lax.Precision.HIGHEST)
    total = jnp.zeros_like(extended)
    total = total.at[:, :, right_cells].add(weights * jnp.take(from_left, left_cells, axis=2))
    total = total.at[:, :, left_cells].add(weights * jnp.take(from_right, right_cells, axis=2))
    return total[:, :, :owned]


def reference(adjoint_seed, inv_blocks, flux_jacobians, modal_shapes, modal_gain, face_cells, face_weights, colours, send_cells):
    parts = N_CELL

    def split(array):
        shaped = array.reshape(array.shape[:-1] + (parts, array.shape[-1] // parts))
        return jnp.moveaxis(shaped, -2, 0)

    seed_p = split(adjoint_seed)
    inv_p = split(inv_blocks).astype(jnp.float32)
    shapes_p = split(modal_shapes)
    faces_p = split(face_cells)
    weights_p = split(face_weights)
    colour_p = split(colours)
    sends_p = split(send_cells)
    spectral = spectral_matrix(NI)
    owned = CELLS_DEV

    def modal(state):
        return jnp.einsum('pnvc,pmvc->nm', state, shapes_p, precision=lax.Precision.HIGHEST)

    state = jnp.zeros_like(seed_p)
    for sweep in range(ITERS):
        lam = modal(state) * modal_gain[None, :]
        base = seed_p + jnp.einsum('nm,pmvc->pnvc', lam, shapes_p, precision=lax.Precision.HIGHEST)
        sent = jax.vmap(lambda field, lists: jnp.take(field, lists, axis=2))(state, sends_p)
        from_lower = jnp.roll(sent[:, :, :, 1, :], 1, axis=0)
        from_upper = jnp.roll(sent[:, :, :, 0, :], -1, axis=0)
        ghosts = jnp.concatenate([from_lower, from_upper], axis=-1)
        for colour in range(2):
            extended = jnp.concatenate([state, ghosts], axis=-1)
            coupled = jax.vmap(off_product, (0, None, 0, 0, None))(extended, flux_jacobians, faces_p, weights_p, owned)
            spectral_term = frequency * jnp.einsum('mn,pmvc->pnvc', spectral, state, precision=lax.Precision.HIGHEST)
            resid = base - coupled - spectral_term
            updated = jnp.sum(inv_p * resid[:, :, :, None, :], axis=2)
            state = jnp.where(colour_p[:, None, None, :] == colour, updated, state)
    partials = modal(state)
    merged = jnp.moveaxis(state, 0, -2).reshape(adjoint_seed.shape)
    return merged, partials
```

```python
import functools
import math

import jax
import jax.numpy as jnp
from jax import lax
from jax.experimental import pallas as pl
from jax.experimental.pallas import tpu as pltpu
from jax.sharding import PartitionSpec as P

ITERS = 4
FREQUENCY = 0.04
F32 = jnp.float32
BF16 = jnp.bfloat16
MODE_ROWS = 32
CANDIDATES = 64


def spectral_weights(count):
    return [FREQUENCY * 0.5 * (-1.0) ** d / math.tan(math.pi * d / count) for d in range(1, count)]


def bf16_factors(value):
    best_p = value.astype(BF16).astype(F32)
    best_q = jnp.ones_like(value)
    best = jnp.abs(value - best_p)
    for k in range(1, CANDIDATES):
        q = 1.0 + k / 128.0
        p = (value * (1.0 / q)).astype(BF16).astype(F32)
        miss = jnp.abs(value - p * q)
        better = miss < best
        best = jnp.where(better, miss, best)
        best_p = jnp.where(better, p, best_p)
        best_q = jnp.where(better, q, best_q)
    return best_p.astype(BF16), best_q.astype(BF16)


def split(value):
    high = value.astype(BF16)
    return high, (value - high.astype(F32)).astype(BF16)


def mm(left, right):
    return jnp.dot(left, right, preferred_element_type=F32)


def mm_nt(left, right):
    return lax.dot_general(left, right, (((1,), (1,)), ((), ())), preferred_element_type=F32)


def kernel(
    n,
    seed_hbm,
    inv_hbm,
    flux_ref,
    shapes_hbm,
    gain_ref,
    faces_ref,
    g_ref,
    col_ref,
    send_ref,
    out_hbm,
    part_ref,
    seed_ref,
    inv_ref,
    shapes_ref,
    w_ref,
    gain_pad,
    left_hot,
    right_hot,
    upper_hot,
    m_high,
    m_low,
    mg_high,
    mg_low,
    p_ref,
    sel_ref,
    x_ref,
    z_ref,
    base_ref,
    ab_ref,
    q_all,
    ghost_out,
    ghost_in,
    in_sem,
    q_send,
    q_recv,
    g_send,
    g_recv,
):
    nvar, count, owned = seed_ref.shape
    modes = shapes_ref.shape[1]
    rows = count * nvar
    halo = send_ref.shape[1]
    nfaces = faces_ref.shape[1]
    me = lax.axis_index("cell")
    lower, upper = lax.rem(me + n - 1, n), lax.rem(me + 1, n)
    peers = partners(me, n)
    loads = [
        pltpu.make_async_copy(src, dst, in_sem.at[k])
        for k, (src, dst) in enumerate(
            [(seed_hbm, seed_ref), (shapes_hbm, shapes_ref), (inv_hbm, inv_ref)]
        )
    ]
    for load in loads:
        load.start()

    barrier = pltpu.get_barrier_semaphore()
    for d in range(1, n):
        pl.semaphore_signal(barrier, inc=1, device_id={"cell": peers[d]}, device_id_type=pl.DeviceIdType.MESH)

    left = faces_ref[0:1, :].astype(jnp.int16)
    right = faces_ref[1:2, :].astype(jnp.int16)
    p_tile, q_tile = bf16_factors(g_ref[...])
    p_tile, q_tile = p_tile.astype(F32), q_tile.astype(F32)
    p_row = jnp.concatenate([p_tile[k : k + 1, :] for k in range(nfaces // 128)], axis=1).astype(BF16)
    q_row = jnp.concatenate([q_tile[k : k + 1, :] for k in range(nfaces // 128)], axis=1).astype(BF16)
    step = 128
    tall = owned + halo

    def hot(index, start, size, value):
        lines = lax.broadcasted_iota(jnp.int32, (size, 128), 0).astype(jnp.int16)
        lines = jnp.concatenate([lines] * (nfaces // 128), axis=1)
        near = jnp.broadcast_to((index.astype(jnp.int32) - start).astype(jnp.int16), (size, nfaces))
        zero = jnp.zeros((size, nfaces), BF16)
        return jnp.where(near == lines, jnp.broadcast_to(value, (size, nfaces)), zero)

    @pl.loop(0, tall // step)
    def _(t):
        at = pl.multiple_of(t * step, step)
        left_hot[pl.ds(at, step), :] = hot(left, at, step, p_row)

    upper_hot[...] = hot(right, owned + halo, halo, q_row)
    wide = 256
    tall_step = owned // 2

    @pl.loop(0, owned // wide)
    def _(t):
        at = pl.multiple_of(t * wide, wide)
        right_now = hot(right, at, wide, q_row)
        right_hot[pl.ds(at, wide), :] = right_now
        for part in range(owned // tall_step):
            r0 = part * tall_step
            high, low = split(mm_nt(left_hot[r0 : r0 + tall_step, :], right_now))
            m_high[r0 : r0 + tall_step, pl.ds(at, wide)] = high
            m_low[r0 : r0 + tall_step, pl.ds(at, wide)] = low

    def build_ghost_matrix():
        @pl.loop(0, owned // wide)
        def _(t):
            at = pl.multiple_of(t * wide, wide)
            high, low = split(mm_nt(left_hot[owned:tall, :], right_hot[pl.ds(at, wide), :]))
            mg_high[0:halo, pl.ds(at, wide)] = high
            mg_low[0:halo, pl.ds(at, wide)] = low
            high, low = split(mm_nt(upper_hot[...], left_hot[pl.ds(at, wide), :]))
            mg_high[halo:, pl.ds(at, wide)] = high
            mg_low[halo:, pl.ds(at, wide)] = low

    eye_line = lax.broadcasted_iota(jnp.int32, (count, rows), 0)
    eye_lane = lax.broadcasted_iota(jnp.int32, (count, rows), 1)
    eye = lax.rem(eye_lane, count) == eye_line
    blocks = []
    for side in range(2):
        for w in range(nvar):
            row = jnp.concatenate([flux_ref[v, w][side : side + 1, :] for v in range(nvar)], axis=1)
            blocks.append(jnp.where(eye, jnp.broadcast_to(row, (count, rows)), 0.0))
    line = lax.broadcasted_iota(jnp.int32, (rows, rows), 0)
    lane = lax.broadcasted_iota(jnp.int32, (rows, rows), 1)
    apart = lax.rem(lane, count) - lax.rem(line, count)
    spectral = jnp.zeros((rows, rows), F32)
    for d, weight in enumerate(spectral_weights(count), 1):
        spectral = jnp.where(apart == d, weight, jnp.where(apart == -d, -weight, spectral))
    spectral = jnp.where(lax.div(lane, count) == lax.div(line, count), spectral, 0.0)
    w_high, w_low = split(jnp.concatenate(blocks + [spectral], axis=0))
    lane = lax.broadcasted_iota(jnp.int32, (rows, 3 * rows), 1)
    line = lax.broadcasted_iota(jnp.int32, (rows, 3 * rows), 0)
    first = jnp.where((lane == line) | (lane == line + rows), 1.0, 0.0).astype(BF16)
    last = jnp.where(lane == line + 2 * rows, 1.0, 0.0).astype(BF16)
    w_ref[...] = (mm(w_high, first) + mm(w_low, last)).astype(BF16)
    for load in loads:
        load.wait()
    gain_pad[...] = jnp.zeros((1, 128), F32)
    gain_pad[:, 0:modes] = gain_ref[...]
    send_row = jnp.concatenate([send_ref[0:1, :], send_ref[1:2, :]], axis=1)
    sel_ref[...] = jnp.where(
        send_row == lax.broadcasted_iota(jnp.int32, (owned, 2 * halo), 0), 1.0, 0.0
    ).astype(BF16)
    for v in range(nvar):
        shape_v = shapes_ref[v]
        shape_v = jnp.concatenate([shape_v, jnp.zeros((MODE_ROWS - modes, owned), F32)], axis=0)
        high, low = split(shape_v)
        p_ref[v, 0:MODE_ROWS, :] = high
        p_ref[v, MODE_ROWS:, :] = low
        z_ref[v * count : (v + 1) * count, :] = seed_ref[v]
    colours = col_ref[...]

    def update(colour):
        mask = colours == colour
        for w in range(nvar):
            spot = slice(w * count, (w + 1) * count)
            total = inv_ref[0, w].astype(F32) * z_ref[0:count, :]
            for v in range(1, nvar):
                total = total + inv_ref[v, w].astype(F32) * z_ref[v * count : (v + 1) * count, :]
            x_ref[spot, :] = jnp.where(mask, total, x_ref[spot, :])

    def coupling():
        high, low = split(x_ref[...])
        both = mm(w_ref[...], jnp.concatenate([high, low, high], axis=0))
        a_high, a_low = split(both[:rows])
        b_high, b_low = split(both[rows : 2 * rows])
        ab_ref[0, 0:rows, :] = a_high
        ab_ref[0, rows:, :] = a_low
        ab_ref[1, 0:rows, :] = b_high
        ab_ref[1, rows:, :] = b_low
        z_ref[...] = both[2 * rows :]

        @pl.loop(0, owned // wide)
        def _(t):
            at = pl.multiple_of(t * wide, wide)
            cols = pl.ds(at, wide)
            one = mm(ab_ref[0], m_high[:, cols]) + mm_nt(ab_ref[1], m_high[cols, :])
            two = mm(ab_ref[0, 0:rows, :], m_low[:, cols]) + mm_nt(ab_ref[1, 0:rows, :], m_low[cols, :])
            z_ref[:, cols] = z_ref[:, cols] + (one[:rows] + one[rows:] + two)

    def modal_copies(turn):
        return [
            pltpu.make_async_remote_copy(
                src_ref=q_all.at[turn, me],
                dst_ref=q_all.at[turn, me],
                send_sem=q_send.at[turn, d],
                recv_sem=q_recv.at[turn, d],
                device_id={"cell": peers[d]},
                device_id_type=pl.DeviceIdType.MESH,
            )
            for d in range(n - 1, 0, -1)
        ]

    def ghost_copies(turn):
        return [
            pltpu.make_async_remote_copy(
                src_ref=ghost_out.at[turn, way],
                dst_ref=ghost_in.at[turn, 1 - way],
                send_sem=g_send.at[turn, way],
                recv_sem=g_recv.at[turn, way],
                device_id={"cell": lower if way == 0 else upper},
                device_id_type=pl.DeviceIdType.MESH,
            )
            for way in range(2)
        ]

    def start_exchange(turn):
        high, low = split(x_ref[...])
        copies = []
        if turn < ITERS - 1:
            picked = mm(jnp.concatenate([high, low], axis=0), sel_ref[...])
            picked = picked[:rows] + picked[rows:]
            ghost_out[turn, 0] = picked[:, :halo]
            ghost_out[turn, 1] = picked[:, halo:]
            copies = ghost_copies(turn)
            if turn == 0:
                pl.semaphore_wait(barrier, n - 1)
            for copy in copies:
                copy.start()
        gram = jnp.zeros((2 * count, 2 * MODE_ROWS), F32)
        for v in range(nvar):
            spot = slice(v * count, (v + 1) * count)
            gram = gram + mm_nt(jnp.concatenate([high[spot], low[spot]], axis=0), p_ref[v])
        gram = gram[:count] + gram[count:]
        part = gram[:, :MODE_ROWS] + gram[:, MODE_ROWS:]
        half = count // 2
        q_all[turn, me] = jnp.concatenate(
            [part[:half], part[half:], jnp.zeros((half, 128 - 2 * MODE_ROWS), F32)], axis=1
        )
        modal = modal_copies(turn)
        for copy in modal:
            copy.start()
        return copies + modal

    def modal_sum(turn):
        total = q_all[turn, 0]
        for d in range(1, n):
            total = total + q_all[turn, d]
        return jnp.concatenate([total[:, :MODE_ROWS], total[:, MODE_ROWS : 2 * MODE_ROWS]], axis=0)

    x_ref[...] = jnp.zeros((rows, owned), F32)
    update(0)
    coupling()
    for v in range(nvar):
        spot = slice(v * count, (v + 1) * count)
        z_ref[spot, :] = seed_ref[v] - z_ref[spot, :]
    update(1)
    copies = start_exchange(0)
    build_ghost_matrix()
    for sweep in range(1, ITERS):
        coupling()
        for copy in copies:
            copy.wait()
        low_part = ghost_in[sweep - 1, 0]
        up_part = ghost_in[sweep - 1, 1]
        high, low = split(jnp.concatenate([low_part, up_part], axis=1))
        both = mm(w_ref[0 : 2 * rows, :], jnp.concatenate([high, low, high], axis=0))
        ghost_ab = jnp.concatenate([both[:rows, :halo], both[rows:, halo:]], axis=1)
        high, low = split(ghost_ab)
        term = mm(jnp.concatenate([high, low], axis=0), mg_high[...])
        term = term[:rows] + term[rows:] + mm(high, mg_low[...])
        lam = modal_sum(sweep - 1)[:, :MODE_ROWS] * gain_pad[:, :MODE_ROWS]
        lam_high, lam_low = split(lam)
        lam_both = jnp.concatenate([lam_high, lam_low], axis=0)
        for v in range(nvar):
            spot = slice(v * count, (v + 1) * count)
            lift = mm(lam_both, p_ref[v, 0:MODE_ROWS, :])
            lift = lift[:count] + lift[count:] + mm(lam_high, p_ref[v, MODE_ROWS:, :])
            base = seed_ref[v] + lift - term[spot]
            base_ref[spot, :] = base
            z_ref[spot, :] = base - z_ref[spot, :]
        update(0)
        coupling()
        z_ref[...] = base_ref[...] - z_ref[...]
        update(1)
        copies = start_exchange(sweep)
    store = pltpu.make_async_copy(x_ref, out_hbm, in_sem.at[0])
    store.start()
    for copy in copies:
        copy.wait()
    part_ref[...] = modal_sum(ITERS - 1)[:, :modes]
    store.wait()


def partners(me, n):
    if n & (n - 1):
        return [lax.rem(me + d, n) for d in range(n)]
    places = []
    for d in range(n):
        place = me
        bit = 1
        while bit < n:
            if d & bit:
                place = place + bit - 2 * bit * lax.rem(lax.div(me, bit), 2)
            bit *= 2
        places.append(place)
    return places


def hand_over(out_ref, part_ref, out_final, part_final, sem):
    first = pltpu.make_async_copy(out_ref, out_final, sem.at[0])
    second = pltpu.make_async_copy(part_ref, part_final, sem.at[1])
    first.start()
    second.start()
    first.wait()
    second.wait()


def local(
    adjoint_seed,
    inv_blocks,
    flux_jacobians,
    modal_shapes,
    modal_gain,
    face_cells,
    face_weights,
    colours,
    send_cells,
):
    n = lax.axis_size("cell")
    count, nvar, owned = adjoint_seed.shape
    modes = modal_shapes.shape[0]
    rows = count * nvar
    halo = send_cells.shape[1]
    nfaces = face_weights.shape[0]
    inverse = jnp.transpose(inv_blocks, (1, 2, 0, 3))
    vmem = pl.BlockSpec(memory_space=pltpu.VMEM)
    hbm = pl.BlockSpec(memory_space=pl.ANY)
    tall = owned + halo
    turns = ITERS
    out, part = pl.pallas_call(
        functools.partial(kernel, n),
        out_shape=(
            jax.ShapeDtypeStruct((rows, owned), F32),
            jax.ShapeDtypeStruct((count, modes), F32),
        ),
        in_specs=[hbm, hbm, vmem, hbm] + [vmem] * 5,
        out_specs=(hbm, vmem),
        scratch_shapes=[
            pltpu.VMEM((nvar, count, owned), F32),
            pltpu.VMEM((nvar, nvar, count, owned), BF16),
            pltpu.VMEM((nvar, modes, owned), F32),
            pltpu.VMEM((3 * rows, 3 * rows), BF16),
            pltpu.VMEM((1, 128), F32),
            pltpu.VMEM((tall, nfaces), BF16),
            pltpu.VMEM((owned, nfaces), BF16),
            pltpu.VMEM((halo, nfaces), BF16),
            pltpu.VMEM((owned, owned), BF16),
            pltpu.VMEM((owned, owned), BF16),
            pltpu.VMEM((2 * halo, owned), BF16),
            pltpu.VMEM((2 * halo, owned), BF16),
            pltpu.VMEM((nvar, 2 * MODE_ROWS, owned), BF16),
            pltpu.VMEM((owned, 2 * halo), BF16),
            pltpu.VMEM((rows, owned), F32),
            pltpu.VMEM((rows, owned), F32),
            pltpu.VMEM((rows, owned), F32),
            pltpu.VMEM((2, 2 * rows, owned), BF16),
            pltpu.VMEM((turns, n, count // 2, 128), F32),
            pltpu.VMEM((turns - 1, 2, rows, halo), F32),
            pltpu.VMEM((turns - 1, 2, rows, halo), F32),
            pltpu.SemaphoreType.DMA((3,)),
            pltpu.SemaphoreType.DMA((turns, n)),
            pltpu.SemaphoreType.DMA((turns, n)),
            pltpu.SemaphoreType.DMA((turns - 1, 2)),
            pltpu.SemaphoreType.DMA((turns - 1, 2)),
        ],
        compiler_params=pltpu.CompilerParams(
            collective_id=0, has_side_effects=True, vmem_limit_bytes=56 * 1024 * 1024
        ),
    )(
        jnp.transpose(adjoint_seed, (1, 0, 2)),
        inverse,
        jnp.transpose(flux_jacobians, (2, 3, 0, 1)),
        jnp.transpose(modal_shapes, (1, 0, 2)),
        modal_gain[None, :],
        face_cells,
        face_weights.reshape(nfaces // 128, 128),
        colours[None, :],
        send_cells,
    )
    out, part = pl.pallas_call(
        hand_over,
        out_shape=(
            jax.ShapeDtypeStruct((rows, owned), F32),
            jax.ShapeDtypeStruct((count, modes), F32),
        ),
        in_specs=[hbm, hbm],
        out_specs=(hbm, hbm),
        scratch_shapes=[pltpu.SemaphoreType.DMA((2,))],
    )(out, part)
    return jnp.transpose(out.reshape(nvar, count, owned), (1, 0, 2)), part


def solution(mesh):
    return jax.shard_map(
        local,
        mesh=mesh,
        in_specs=(
            P("group", None, "cell"),
            P("group", None, None, "cell"),
            P(None, "group", None, None),
            P(None, None, "cell"),
            P("group"),
            P(None, "cell"),
            P("cell"),
            P("cell"),
            P(None, "cell"),
        ),
        out_specs=(P("group", None, "cell"), P("group", None)),
        check_vma=False,
    )
```

```python
import functools
import math

import jax
import jax.numpy as jnp
from jax import lax
from jax.experimental import pallas as pl
from jax.experimental.pallas import tpu as pltpu
from jax.sharding import PartitionSpec as P

ITERS = 4
FREQUENCY = 0.04
F32 = jnp.float32
BF16 = jnp.bfloat16
MODE_ROWS = 32
CANDIDATES = 64


def spectral_weights(count):
    return [FREQUENCY * 0.5 * (-1.0) ** d / math.tan(math.pi * d / count) for d in range(1, count)]


def bf16_factors(value):
    best_p = value.astype(BF16).astype(F32)
    best_q = jnp.ones_like(value)
    best = jnp.abs(value - best_p)
    for k in range(1, CANDIDATES):
        q = 1.0 + k / 128.0
        p = (value * (1.0 / q)).astype(BF16).astype(F32)
        miss = jnp.abs(value - p * q)
        better = miss < best
        best = jnp.where(better, miss, best)
        best_p = jnp.where(better, p, best_p)
        best_q = jnp.where(better, q, best_q)
    return best_p.astype(BF16), best_q.astype(BF16)


def split(value):
    high = value.astype(BF16)
    return high, (value - high.astype(F32)).astype(BF16)


def mm(left, right):
    return jnp.dot(left, right, preferred_element_type=F32)


def mm_nt(left, right):
    return lax.dot_general(left, right, (((1,), (1,)), ((), ())), preferred_element_type=F32)


def kernel(
    n,
    seed_hbm,
    inv_hbm,
    flux_ref,
    shapes_hbm,
    gain_ref,
    faces_ref,
    g_ref,
    col_ref,
    send_ref,
    out_hbm,
    part_ref,
    seed_ref,
    inv_ref,
    shapes_ref,
    w_ref,
    gain_pad,
    left_hot,
    right_hot,
    upper_hot,
    m_high,
    m_low,
    mg_high,
    mg_low,
    p_ref,
    sel_ref,
    x_ref,
    z_ref,
    base_ref,
    ab_ref,
    q_all,
    ghost_out,
    ghost_in,
    in_sem,
    q_send,
    q_recv,
    g_send,
    g_recv,
):
    nvar, count, owned = seed_ref.shape
    modes = shapes_ref.shape[1]
    rows = count * nvar
    halo = send_ref.shape[1]
    nfaces = faces_ref.shape[1]
    me = lax.axis_index("cell")
    lower, upper = lax.rem(me + n - 1, n), lax.rem(me + 1, n)
    peers = partners(me, n)
    loads = [
        pltpu.make_async_copy(src, dst, in_sem.at[k])
        for k, (src, dst) in enumerate(
            [(seed_hbm, seed_ref), (shapes_hbm, shapes_ref), (inv_hbm, inv_ref)]
        )
    ]
    for load in loads:
        load.start()

    barrier = pltpu.get_barrier_semaphore()
    for d in range(1, n):
        pl.semaphore_signal(barrier, inc=1, device_id={"cell": peers[d]}, device_id_type=pl.DeviceIdType.MESH)

    left = faces_ref[0:1, :].astype(jnp.int16)
    right = faces_ref[1:2, :].astype(jnp.int16)
    p_tile, q_tile = bf16_factors(g_ref[...])
    p_tile, q_tile = p_tile.astype(F32), q_tile.astype(F32)
    p_row = jnp.concatenate([p_tile[k : k + 1, :] for k in range(nfaces // 128)], axis=1).astype(BF16)
    q_row = jnp.concatenate([q_tile[k : k + 1, :] for k in range(nfaces // 128)], axis=1).astype(BF16)
    step = 128
    tall = owned + halo

    def hot(index, start, size, value):
        lines = lax.broadcasted_iota(jnp.int32, (size, 128), 0).astype(jnp.int16)
        lines = jnp.concatenate([lines] * (nfaces // 128), axis=1)
        near = jnp.broadcast_to((index.astype(jnp.int32) - start).astype(jnp.int16), (size, nfaces))
        zero = jnp.zeros((size, nfaces), BF16)
        return jnp.where(near == lines, jnp.broadcast_to(value, (size, nfaces)), zero)

    @pl.loop(0, tall // step)
    def _(t):
        at = pl.multiple_of(t * step, step)
        left_hot[pl.ds(at, step), :] = hot(left, at, step, p_row)

    upper_hot[...] = hot(right, owned + halo, halo, q_row)
    wide = 256
    broad = 1024
    tall_step = owned // 2

    @pl.loop(0, owned // wide)
    def _(t):
        at = pl.multiple_of(t * wide, wide)
        right_now = hot(right, at, wide, q_row)
        right_hot[pl.ds(at, wide), :] = right_now
        for part in range(owned // tall_step):
            r0 = part * tall_step
            high, low = split(mm_nt(left_hot[r0 : r0 + tall_step, :], right_now))
            m_high[r0 : r0 + tall_step, pl.ds(at, wide)] = high
            m_low[r0 : r0 + tall_step, pl.ds(at, wide)] = low

    def build_ghost_matrix():
        @pl.loop(0, owned // wide)
        def _(t):
            at = pl.multiple_of(t * wide, wide)
            high, low = split(mm_nt(left_hot[owned:tall, :], right_hot[pl.ds(at, wide), :]))
            mg_high[0:halo, pl.ds(at, wide)] = high
            mg_low[0:halo, pl.ds(at, wide)] = low
            high, low = split(mm_nt(upper_hot[...], left_hot[pl.ds(at, wide), :]))
            mg_high[halo:, pl.ds(at, wide)] = high
            mg_low[halo:, pl.ds(at, wide)] = low

    eye_line = lax.broadcasted_iota(jnp.int32, (count, rows), 0)
    eye_lane = lax.broadcasted_iota(jnp.int32, (count, rows), 1)
    eye = lax.rem(eye_lane, count) == eye_line
    blocks = []
    for side in range(2):
        for w in range(nvar):
            row = jnp.concatenate([flux_ref[v, w][side : side + 1, :] for v in range(nvar)], axis=1)
            blocks.append(jnp.where(eye, jnp.broadcast_to(row, (count, rows)), 0.0))
    line = lax.broadcasted_iota(jnp.int32, (rows, rows), 0)
    lane = lax.broadcasted_iota(jnp.int32, (rows, rows), 1)
    apart = lax.rem(lane, count) - lax.rem(line, count)
    spectral = jnp.zeros((rows, rows), F32)
    for d, weight in enumerate(spectral_weights(count), 1):
        spectral = jnp.where(apart == d, weight, jnp.where(apart == -d, -weight, spectral))
    spectral = jnp.where(lax.div(lane, count) == lax.div(line, count), spectral, 0.0)
    w_high, w_low = split(jnp.concatenate(blocks + [spectral], axis=0))
    lane = lax.broadcasted_iota(jnp.int32, (rows, 3 * rows), 1)
    line = lax.broadcasted_iota(jnp.int32, (rows, 3 * rows), 0)
    first = jnp.where((lane == line) | (lane == line + rows), 1.0, 0.0).astype(BF16)
    last = jnp.where(lane == line + 2 * rows, 1.0, 0.0).astype(BF16)
    w_ref[...] = (mm(w_high, first) + mm(w_low, last)).astype(BF16)
    for load in loads:
        load.wait()
    gain_pad[...] = jnp.zeros((1, 128), F32)
    gain_pad[:, 0:modes] = gain_ref[...]
    send_row = jnp.concatenate([send_ref[0:1, :], send_ref[1:2, :]], axis=1)
    sel_ref[...] = jnp.where(
        send_row == lax.broadcasted_iota(jnp.int32, (owned, 2 * halo), 0), 1.0, 0.0
    ).astype(BF16)
    for v in range(nvar):
        shape_v = shapes_ref[v]
        shape_v = jnp.concatenate([shape_v, jnp.zeros((MODE_ROWS - modes, owned), F32)], axis=0)
        high, low = split(shape_v)
        p_ref[v, 0:MODE_ROWS, :] = high
        p_ref[v, MODE_ROWS:, :] = low
        z_ref[v * count : (v + 1) * count, :] = seed_ref[v]
    colours = col_ref[...]

    def update(colour):
        mask = colours == colour
        for w in range(nvar):
            spot = slice(w * count, (w + 1) * count)
            total = inv_ref[0, w].astype(F32) * z_ref[0:count, :]
            for v in range(1, nvar):
                total = total + inv_ref[v, w].astype(F32) * z_ref[v * count : (v + 1) * count, :]
            x_ref[spot, :] = jnp.where(mask, total, x_ref[spot, :])

    def coupling():
        high, low = split(x_ref[...])
        both = mm(w_ref[...], jnp.concatenate([high, low, high], axis=0))
        a_high, a_low = split(both[:rows])
        b_high, b_low = split(both[rows : 2 * rows])
        ab_ref[0, 0:rows, :] = a_high
        ab_ref[0, rows:, :] = a_low
        ab_ref[1, 0:rows, :] = b_high
        ab_ref[1, rows:, :] = b_low
        z_ref[...] = both[2 * rows :]

        @pl.loop(0, owned // broad)
        def _(t):
            at = pl.multiple_of(t * broad, broad)
            cols = pl.ds(at, broad)
            one = mm(ab_ref[0], m_high[:, cols]) + mm_nt(ab_ref[1], m_high[cols, :])
            two = mm(ab_ref[0, 0:rows, :], m_low[:, cols]) + mm_nt(ab_ref[1, 0:rows, :], m_low[cols, :])
            z_ref[:, cols] = z_ref[:, cols] + (one[:rows] + one[rows:] + two)

    def modal_copies(turn):
        return [
            pltpu.make_async_remote_copy(
                src_ref=q_all.at[turn, me],
                dst_ref=q_all.at[turn, me],
                send_sem=q_send.at[turn, d],
                recv_sem=q_recv.at[turn, d],
                device_id={"cell": peers[d]},
                device_id_type=pl.DeviceIdType.MESH,
            )
            for d in range(n - 1, 0, -1)
        ]

    def ghost_copies(turn):
        return [
            pltpu.make_async_remote_copy(
                src_ref=ghost_out.at[turn, way],
                dst_ref=ghost_in.at[turn, 1 - way],
                send_sem=g_send.at[turn, way],
                recv_sem=g_recv.at[turn, way],
                device_id={"cell": lower if way == 0 else upper},
                device_id_type=pl.DeviceIdType.MESH,
            )
            for way in range(2)
        ]

    def start_exchange(turn):
        high, low = split(x_ref[...])

        @pl.when(turn < ITERS - 1)
        def _():
            picked = mm(jnp.concatenate([high, low], axis=0), sel_ref[...])
            picked = picked[:rows] + picked[rows:]
            ghost_out[turn, 0] = picked[:, :halo]
            ghost_out[turn, 1] = picked[:, halo:]

            @pl.when(turn == 0)
            def _():
                pl.semaphore_wait(barrier, n - 1)

            for copy in ghost_copies(turn):
                copy.start()

        gram = jnp.zeros((2 * count, 2 * MODE_ROWS), F32)
        for v in range(nvar):
            spot = slice(v * count, (v + 1) * count)
            gram = gram + mm_nt(jnp.concatenate([high[spot], low[spot]], axis=0), p_ref[v])
        gram = gram[:count] + gram[count:]
        part = gram[:, :MODE_ROWS] + gram[:, MODE_ROWS:]
        half = count // 2
        q_all[turn, me] = jnp.concatenate(
            [part[:half], part[half:], jnp.zeros((half, 128 - 2 * MODE_ROWS), F32)], axis=1
        )
        for copy in modal_copies(turn):
            copy.start()

    def modal_sum(turn):
        total = q_all[turn, 0]
        for d in range(1, n):
            total = total + q_all[turn, d]
        return jnp.concatenate([total[:, :MODE_ROWS], total[:, MODE_ROWS : 2 * MODE_ROWS]], axis=0)

    x_ref[...] = jnp.zeros((rows, owned), F32)
    for v in range(nvar):
        base_ref[v * count : (v + 1) * count, :] = seed_ref[v]

    @pl.loop(0, ITERS)
    def _(sweep):
        @pl.when(sweep > 0)
        def _():
            coupling()

            @pl.when(sweep == 1)
            def _():
                build_ghost_matrix()

            for copy in ghost_copies(sweep - 1) + modal_copies(sweep - 1):
                copy.wait()
            low_part = ghost_in[sweep - 1, 0]
            up_part = ghost_in[sweep - 1, 1]
            high, low = split(jnp.concatenate([low_part, up_part], axis=1))
            both = mm(w_ref[0 : 2 * rows, :], jnp.concatenate([high, low, high], axis=0))
            ghost_ab = jnp.concatenate([both[:rows, :halo], both[rows:, halo:]], axis=1)
            high, low = split(ghost_ab)
            term = mm(jnp.concatenate([high, low], axis=0), mg_high[...])
            term = term[:rows] + term[rows:] + mm(high, mg_low[...])
            lam = modal_sum(sweep - 1)[:, :MODE_ROWS] * gain_pad[:, :MODE_ROWS]
            lam_high, lam_low = split(lam)
            lam_both = jnp.concatenate([lam_high, lam_low], axis=0)
            for v in range(nvar):
                spot = slice(v * count, (v + 1) * count)
                lift = mm(lam_both, p_ref[v, 0:MODE_ROWS, :])
                lift = lift[:count] + lift[count:] + mm(lam_high, p_ref[v, MODE_ROWS:, :])
                base = seed_ref[v] + lift - term[spot]
                base_ref[spot, :] = base
                z_ref[spot, :] = base - z_ref[spot, :]

        update(0)
        coupling()
        z_ref[...] = base_ref[...] - z_ref[...]
        update(1)
        start_exchange(sweep)

    store = pltpu.make_async_copy(x_ref, out_hbm, in_sem.at[0])
    store.start()
    for copy in modal_copies(ITERS - 1):
        copy.wait()
    part_ref[...] = modal_sum(ITERS - 1)[:, :modes]
    store.wait()


def partners(me, n):
    if n & (n - 1):
        return [lax.rem(me + d, n) for d in range(n)]
    places = []
    for d in range(n):
        place = me
        bit = 1
        while bit < n:
            if d & bit:
                place = place + bit - 2 * bit * lax.rem(lax.div(me, bit), 2)
            bit *= 2
        places.append(place)
    return places


def hand_over(out_ref, part_ref, out_final, part_final, stage, small, sem):
    pieces = 5
    size = out_ref.shape[0] // pieces
    spots = [pl.ds(k * size, size) for k in range(pieces)]
    ins = [pltpu.make_async_copy(out_ref.at[s], stage.at[s], sem.at[0, k]) for k, s in enumerate(spots)]
    outs = [pltpu.make_async_copy(stage.at[s], out_final.at[s], sem.at[1, k]) for k, s in enumerate(spots)]
    ins.append(pltpu.make_async_copy(part_ref, small, sem.at[0, pieces]))
    outs.append(pltpu.make_async_copy(small, part_final, sem.at[1, pieces]))
    for copy in ins:
        copy.start()
    for first, second in zip(ins, outs):
        first.wait()
        second.start()
    for copy in outs:
        copy.wait()


def local(
    adjoint_seed,
    inv_blocks,
    flux_jacobians,
    modal_shapes,
    modal_gain,
    face_cells,
    face_weights,
    colours,
    send_cells,
):
    n = lax.axis_size("cell")
    count, nvar, owned = adjoint_seed.shape
    modes = modal_shapes.shape[0]
    rows = count * nvar
    halo = send_cells.shape[1]
    nfaces = face_weights.shape[0]
    inverse = jnp.transpose(inv_blocks, (1, 2, 0, 3))
    vmem = pl.BlockSpec(memory_space=pltpu.VMEM)
    hbm = pl.BlockSpec(memory_space=pl.ANY)
    tall = owned + halo
    turns = ITERS
    out, part = pl.pallas_call(
        functools.partial(kernel, n),
        out_shape=(
            jax.ShapeDtypeStruct((rows, owned), F32),
            jax.ShapeDtypeStruct((count, modes), F32),
        ),
        in_specs=[hbm, hbm, vmem, hbm] + [vmem] * 5,
        out_specs=(hbm, vmem),
        scratch_shapes=[
            pltpu.VMEM((nvar, count, owned), F32),
            pltpu.VMEM((nvar, nvar, count, owned), BF16),
            pltpu.VMEM((nvar, modes, owned), F32),
            pltpu.VMEM((3 * rows, 3 * rows), BF16),
            pltpu.VMEM((1, 128), F32),
            pltpu.VMEM((tall, nfaces), BF16),
            pltpu.VMEM((owned, nfaces), BF16),
            pltpu.VMEM((halo, nfaces), BF16),
            pltpu.VMEM((owned, owned), BF16),
            pltpu.VMEM((owned, owned), BF16),
            pltpu.VMEM((2 * halo, owned), BF16),
            pltpu.VMEM((2 * halo, owned), BF16),
            pltpu.VMEM((nvar, 2 * MODE_ROWS, owned), BF16),
            pltpu.VMEM((owned, 2 * halo), BF16),
            pltpu.VMEM((rows, owned), F32),
            pltpu.VMEM((rows, owned), F32),
            pltpu.VMEM((rows, owned), F32),
            pltpu.VMEM((2, 2 * rows, owned), BF16),
            pltpu.VMEM((turns, n, count // 2, 128), F32),
            pltpu.VMEM((turns - 1, 2, rows, halo), F32),
            pltpu.VMEM((turns - 1, 2, rows, halo), F32),
            pltpu.SemaphoreType.DMA((3,)),
            pltpu.SemaphoreType.DMA((turns, n)),
            pltpu.SemaphoreType.DMA((turns, n)),
            pltpu.SemaphoreType.DMA((turns - 1, 2)),
            pltpu.SemaphoreType.DMA((turns - 1, 2)),
        ],
        compiler_params=pltpu.CompilerParams(
            collective_id=0, has_side_effects=True, vmem_limit_bytes=56 * 1024 * 1024
        ),
    )(
        jnp.transpose(adjoint_seed, (1, 0, 2)),
        inverse,
        jnp.transpose(flux_jacobians, (2, 3, 0, 1)),
        jnp.transpose(modal_shapes, (1, 0, 2)),
        modal_gain[None, :],
        face_cells,
        face_weights.reshape(nfaces // 128, 128),
        colours[None, :],
        send_cells,
    )
    out, part = pl.pallas_call(
        hand_over,
        out_shape=(
            jax.ShapeDtypeStruct((rows, owned), F32),
            jax.ShapeDtypeStruct((count, modes), F32),
        ),
        in_specs=[hbm, hbm],
        out_specs=(hbm, hbm),
        scratch_shapes=[
            pltpu.VMEM((rows, owned), F32),
            pltpu.VMEM((count, modes), F32),
            pltpu.SemaphoreType.DMA((2, 6)),
        ],
    )(out, part)
    return jnp.transpose(out.reshape(nvar, count, owned), (1, 0, 2)), part


def solution(mesh):
    return jax.shard_map(
        local,
        mesh=mesh,
        in_specs=(
            P("group", None, "cell"),
            P("group", None, None, "cell"),
            P(None, "group", None, None),
            P(None, None, "cell"),
            P("group"),
            P(None, "cell"),
            P("cell"),
            P("cell"),
            P(None, "cell"),
        ),
        out_specs=(P("group", None, "cell"), P("group", None)),
        check_vma=False,
    )
```

```python
import functools
import math

import jax
import jax.numpy as jnp
from jax import lax
from jax.experimental import pallas as pl
from jax.experimental.pallas import tpu as pltpu
from jax.sharding import PartitionSpec as P

ITERS = 4
FREQUENCY = 0.04
F32 = jnp.float32
BF16 = jnp.bfloat16
F8 = jnp.float8_e4m3fn
LIFT = 256.0
F8_MAX = 448.0
SPAN = 32.0
MODE_ROWS = 24
CANDIDATES = 64


def spectral_weights(count):
    return [FREQUENCY * 0.5 * (-1.0) ** d / math.tan(math.pi * d / count) for d in range(1, count)]


def bf16_factors(value):
    best_p = value.astype(BF16).astype(F32)
    best_q = jnp.ones_like(value)
    best = jnp.abs(value - best_p)
    for k in range(1, CANDIDATES):
        q = 1.0 + k / 128.0
        p = (value * (1.0 / q)).astype(BF16).astype(F32)
        miss = jnp.abs(value - p * q)
        better = miss < best
        best = jnp.where(better, miss, best)
        best_p = jnp.where(better, p, best_p)
        best_q = jnp.where(better, q, best_q)
    return best_p.astype(BF16), best_q.astype(BF16)


def split(value):
    high = value.astype(BF16)
    return high, (value - high.astype(F32)).astype(BF16)


def split_f8(value):
    high = value.astype(BF16)
    low = (value - high.astype(F32)) * LIFT
    return high, jnp.clip(low, -F8_MAX, F8_MAX).astype(F8)


def mm(left, right):
    return jnp.dot(left, right, preferred_element_type=F32)


def mm_nt(left, right):
    return lax.dot_general(left, right, (((1,), (1,)), ((), ())), preferred_element_type=F32)


def kernel(
    n,
    seed_hbm,
    inv_hbm,
    flux_ref,
    shapes_hbm,
    gain_ref,
    faces_ref,
    g_ref,
    col_ref,
    send_ref,
    out_hbm,
    part_ref,
    seed_ref,
    inv_ref,
    shapes_ref,
    w_ref,
    gain_pad,
    left_hot,
    right_hot,
    upper_hot,
    m_high,
    m_low,
    t_high,
    t_low,
    mg_high,
    mg_low,
    p_ref,
    sel_ref,
    x_ref,
    z_ref,
    base_ref,
    ab_ref,
    ab_low,
    q_all,
    ghost_out,
    ghost_in,
    in_sem,
    q_send,
    q_recv,
    g_send,
    g_recv,
):
    nvar, count, owned = seed_ref.shape
    modes = shapes_ref.shape[1]
    rows = count * nvar
    halo = send_ref.shape[1]
    nfaces = faces_ref.shape[1]
    me = lax.axis_index("cell")
    lower, upper = lax.rem(me + n - 1, n), lax.rem(me + 1, n)
    peers = partners(me, n)
    loads = [
        pltpu.make_async_copy(src, dst, in_sem.at[k])
        for k, (src, dst) in enumerate(
            [(seed_hbm, seed_ref), (shapes_hbm, shapes_ref), (inv_hbm, inv_ref)]
        )
    ]
    for load in loads:
        load.start()

    barrier = pltpu.get_barrier_semaphore()
    for d in range(1, n):
        pl.semaphore_signal(barrier, inc=1, device_id={"cell": peers[d]}, device_id_type=pl.DeviceIdType.MESH)

    left = faces_ref[0:1, :].astype(jnp.int16)
    right = faces_ref[1:2, :].astype(jnp.int16)
    p_tile, q_tile = bf16_factors(g_ref[...])
    p_tile, q_tile = p_tile.astype(F32), q_tile.astype(F32)
    p_row = jnp.concatenate([p_tile[k : k + 1, :] for k in range(nfaces // 128)], axis=1).astype(BF16)
    q_row = jnp.concatenate([q_tile[k : k + 1, :] for k in range(nfaces // 128)], axis=1).astype(BF16)
    step = 128
    tall = owned + halo

    def hot(index, start, size, value):
        lines = lax.broadcasted_iota(jnp.int32, (size, 128), 0).astype(jnp.int16)
        lines = jnp.concatenate([lines] * (nfaces // 128), axis=1)
        near = jnp.broadcast_to((index.astype(jnp.int32) - start).astype(jnp.int16), (size, nfaces))
        zero = jnp.zeros((size, nfaces), BF16)
        return jnp.where(near == lines, jnp.broadcast_to(value, (size, nfaces)), zero)

    @pl.loop(0, tall // step)
    def _(t):
        at = pl.multiple_of(t * step, step)
        left_hot[pl.ds(at, step), :] = hot(left, at, step, p_row)

    upper_hot[...] = hot(right, owned + halo, halo, q_row)
    wide = 256
    tall_step = owned // 2

    @pl.loop(0, owned // wide)
    def _(t):
        at = pl.multiple_of(t * wide, wide)
        right_now = hot(right, at, wide, q_row)
        right_hot[pl.ds(at, wide), :] = right_now
        for part in range(owned // tall_step):
            r0 = part * tall_step
            block = mm_nt(left_hot[r0 : r0 + tall_step, :], right_now)
            high, low = split_f8(block)
            m_high[r0 : r0 + tall_step, pl.ds(at, wide)] = high
            m_low[r0 : r0 + tall_step, pl.ds(at, wide)] = low
            high, low = split_f8(block.T)
            t_high[pl.ds(at, wide), r0 : r0 + tall_step] = high
            t_low[pl.ds(at, wide), r0 : r0 + tall_step] = low

    def build_ghost_matrix():
        @pl.loop(0, owned // wide)
        def _(t):
            at = pl.multiple_of(t * wide, wide)
            high, low = split(mm_nt(left_hot[owned:tall, :], right_hot[pl.ds(at, wide), :]))
            mg_high[0:halo, pl.ds(at, wide)] = high
            mg_low[0:halo, pl.ds(at, wide)] = low
            high, low = split(mm_nt(upper_hot[...], left_hot[pl.ds(at, wide), :]))
            mg_high[halo:, pl.ds(at, wide)] = high
            mg_low[halo:, pl.ds(at, wide)] = low

    eye_line = lax.broadcasted_iota(jnp.int32, (count, rows), 0)
    eye_lane = lax.broadcasted_iota(jnp.int32, (count, rows), 1)
    eye = lax.rem(eye_lane, count) == eye_line
    blocks = []
    for side in range(2):
        for w in range(nvar):
            row = jnp.concatenate([flux_ref[v, w][side : side + 1, :] for v in range(nvar)], axis=1)
            blocks.append(jnp.where(eye, jnp.broadcast_to(row, (count, rows)), 0.0))
    line = lax.broadcasted_iota(jnp.int32, (rows, rows), 0)
    lane = lax.broadcasted_iota(jnp.int32, (rows, rows), 1)
    apart = lax.rem(lane, count) - lax.rem(line, count)
    spectral = jnp.zeros((rows, rows), F32)
    for d, weight in enumerate(spectral_weights(count), 1):
        spectral = jnp.where(apart == d, weight, jnp.where(apart == -d, -weight, spectral))
    spectral = jnp.where(lax.div(lane, count) == lax.div(line, count), spectral, 0.0)
    w_high, w_low = split(jnp.concatenate(blocks + [spectral], axis=0))
    lane = lax.broadcasted_iota(jnp.int32, (rows, 3 * rows), 1)
    line = lax.broadcasted_iota(jnp.int32, (rows, 3 * rows), 0)
    first = jnp.where((lane == line) | (lane == line + rows), 1.0, 0.0).astype(BF16)
    last = jnp.where(lane == line + 2 * rows, 1.0, 0.0).astype(BF16)
    w_ref[...] = (mm(w_high, first) + mm(w_low, last)).astype(BF16)
    for load in loads:
        load.wait()
    gain_pad[...] = jnp.zeros((1, 128), F32)
    gain_pad[:, 0:modes] = gain_ref[...]
    send_row = jnp.concatenate([send_ref[0:1, :], send_ref[1:2, :]], axis=1)
    sel_ref[:, 0 : 2 * halo] = jnp.where(
        send_row == lax.broadcasted_iota(jnp.int32, (owned, 2 * halo), 0), 1.0, 0.0
    ).astype(BF16)
    pad = jnp.zeros((MODE_ROWS - modes, owned), F32)
    lines = []
    for v in range(nvar):
        lines += [shapes_ref[v], pad]
    lines.append(jnp.zeros((128 - nvar * MODE_ROWS, owned), F32))
    high, low = split(jnp.concatenate(lines, axis=0))
    p_ref[0:128, :] = high
    p_ref[128:256, :] = low
    sel_ref[:, 2 * halo : 2 * halo + 128] = high.astype(F32).T.astype(BF16)
    sel_ref[:, 2 * halo + 128 :] = low.astype(F32).T.astype(BF16)
    for v in range(nvar):
        z_ref[v * count : (v + 1) * count, :] = seed_ref[v]
    colours = col_ref[...]

    def update(colour):
        mask = colours == colour
        for w in range(nvar):
            spot = slice(w * count, (w + 1) * count)
            total = inv_ref[0, w].astype(F32) * z_ref[0:count, :]
            for v in range(1, nvar):
                total = total + inv_ref[v, w].astype(F32) * z_ref[v * count : (v + 1) * count, :]
            x_ref[spot, :] = jnp.where(mask, total, x_ref[spot, :])

    def coupling():
        value = x_ref[...]
        top = jnp.max(jnp.abs(value), axis=0, keepdims=True)
        top = jnp.maximum(jnp.max(top, axis=1, keepdims=True), 1e-30)
        scale = SPAN / top
        high, low = split(value)
        both = mm(w_ref[...], jnp.concatenate([high, low, high], axis=0))
        for side in range(2):
            part = both[side * rows : (side + 1) * rows]
            high, low = split(part)
            ab_ref[side, 0:rows, :] = high
            ab_ref[side, rows:, :] = low
            rough = jnp.concatenate([part * scale, jnp.zeros((96 - rows, owned), F32)], axis=0)
            ab_low[side] = rough.astype(F8)
        one = mm(ab_ref[0], m_high[...]) + mm(ab_ref[1], t_high[...])
        two = mm(ab_low[0], m_low[...]) + mm(ab_low[1], t_low[...])
        z_ref[...] = both[2 * rows :] + (one[:rows] + one[rows:] + two[:rows] * (top * (1.0 / (SPAN * LIFT))))

    def modal_copies(turn):
        return [
            pltpu.make_async_remote_copy(
                src_ref=q_all.at[turn, me],
                dst_ref=q_all.at[turn, me],
                send_sem=q_send.at[turn, d],
                recv_sem=q_recv.at[turn, d],
                device_id={"cell": peers[d]},
                device_id_type=pl.DeviceIdType.MESH,
            )
            for d in range(n - 1, 0, -1)
        ]

    def ghost_copies(turn):
        return [
            pltpu.make_async_remote_copy(
                src_ref=ghost_out.at[turn, way],
                dst_ref=ghost_in.at[turn, 1 - way],
                send_sem=g_send.at[turn, way],
                recv_sem=g_recv.at[turn, way],
                device_id={"cell": lower if way == 0 else upper},
                device_id_type=pl.DeviceIdType.MESH,
            )
            for way in range(2)
        ]

    def start_exchange(turn):
        high, low = split(x_ref[...])
        every = mm(jnp.concatenate([high, low], axis=0), sel_ref[...])
        every = every[:rows] + every[rows:]
        gram = every[:, 2 * halo : 2 * halo + 128] + every[:, 2 * halo + 128 :]
        part = gram[0:count, 0:MODE_ROWS]
        for v in range(1, nvar):
            part = part + gram[v * count : (v + 1) * count, v * MODE_ROWS : (v + 1) * MODE_ROWS]
        half = count // 2
        q_all[turn, me] = jnp.concatenate(
            [part[:half], part[half:], jnp.zeros((half, 128 - 2 * MODE_ROWS), F32)], axis=1
        )

        @pl.when(turn == 0)
        def _():
            pl.semaphore_wait(barrier, n - 1)

        for copy in modal_copies(turn):
            copy.start()

        @pl.when(turn < ITERS - 1)
        def _():
            ghost_out[turn, 0] = every[:, :halo]
            ghost_out[turn, 1] = every[:, halo : 2 * halo]
            for copy in ghost_copies(turn):
                copy.start()

    def modal_sum(turn):
        total = q_all[turn, 0]
        for d in range(1, n):
            total = total + q_all[turn, d]
        return jnp.concatenate([total[:, :MODE_ROWS], total[:, MODE_ROWS : 2 * MODE_ROWS]], axis=0)

    x_ref[...] = jnp.zeros((rows, owned), F32)
    for v in range(nvar):
        base_ref[v * count : (v + 1) * count, :] = seed_ref[v]

    @pl.loop(0, ITERS)
    def _(sweep):
        @pl.when(sweep > 0)
        def _():
            coupling()

            @pl.when(sweep == 1)
            def _():
                build_ghost_matrix()

            for copy in ghost_copies(sweep - 1) + modal_copies(sweep - 1):
                copy.wait()
            low_part = ghost_in[sweep - 1, 0]
            up_part = ghost_in[sweep - 1, 1]
            high, low = split(jnp.concatenate([low_part, up_part], axis=1))
            both = mm(w_ref[0 : 2 * rows, :], jnp.concatenate([high, low, high], axis=0))
            ghost_ab = jnp.concatenate([both[:rows, :halo], both[rows:, halo:]], axis=1)
            ghost_high, ghost_low = split(ghost_ab)
            lam = modal_sum(sweep - 1) * gain_pad[:, :MODE_ROWS]
            lam = jnp.concatenate([lam] * nvar + [jnp.zeros((count, 128 - nvar * MODE_ROWS), F32)], axis=1)
            lam = jnp.concatenate([lam] * nvar, axis=0)
            lane = lax.broadcasted_iota(jnp.int32, (rows, 128), 1)
            line = lax.broadcasted_iota(jnp.int32, (rows, 128), 0)
            lam = jnp.where(lax.div(lane, MODE_ROWS) == lax.div(line, count), -lam, 0.0)
            lam_high, lam_low = split(lam)
            term = mm(jnp.concatenate([ghost_high, ghost_low], axis=0), mg_high[...]) + mm(
                jnp.concatenate([lam_high, lam_low], axis=0), p_ref[0:128, :]
            )
            rest = mm(ghost_high, mg_low[...]) + mm(lam_high, p_ref[128:256, :])
            term = term[:rows] + term[rows:] + rest
            for v in range(nvar):
                spot = slice(v * count, (v + 1) * count)
                base = seed_ref[v] - term[spot]
                base_ref[spot, :] = base
                z_ref[spot, :] = base - z_ref[spot, :]

        update(0)
        coupling()
        z_ref[...] = base_ref[...] - z_ref[...]
        update(1)
        start_exchange(sweep)

    store = pltpu.make_async_copy(x_ref, out_hbm, in_sem.at[0])
    store.start()
    for copy in modal_copies(ITERS - 1):
        copy.wait()
    part_ref[...] = modal_sum(ITERS - 1)[:, :modes]
    store.wait()


def partners(me, n):
    if n & (n - 1):
        return [lax.rem(me + d, n) for d in range(n)]
    places = []
    for d in range(n):
        place = me
        bit = 1
        while bit < n:
            if d & bit:
                place = place + bit - 2 * bit * lax.rem(lax.div(me, bit), 2)
            bit *= 2
        places.append(place)
    return places


def hand_over(out_ref, part_ref, out_final, part_final, stage, small, sem):
    pieces = 5
    size = out_ref.shape[0] // pieces
    spots = [pl.ds(k * size, size) for k in range(pieces)]
    ins = [pltpu.make_async_copy(out_ref.at[s], stage.at[s], sem.at[0, k]) for k, s in enumerate(spots)]
    outs = [pltpu.make_async_copy(stage.at[s], out_final.at[s], sem.at[1, k]) for k, s in enumerate(spots)]
    ins.append(pltpu.make_async_copy(part_ref, small, sem.at[0, pieces]))
    outs.append(pltpu.make_async_copy(small, part_final, sem.at[1, pieces]))
    for copy in ins:
        copy.start()
    for first, second in zip(ins, outs):
        first.wait()
        second.start()
    for copy in outs:
        copy.wait()


def local(
    adjoint_seed,
    inv_blocks,
    flux_jacobians,
    modal_shapes,
    modal_gain,
    face_cells,
    face_weights,
    colours,
    send_cells,
):
    n = lax.axis_size("cell")
    count, nvar, owned = adjoint_seed.shape
    modes = modal_shapes.shape[0]
    rows = count * nvar
    halo = send_cells.shape[1]
    nfaces = face_weights.shape[0]
    inverse = jnp.transpose(inv_blocks, (1, 2, 0, 3))
    vmem = pl.BlockSpec(memory_space=pltpu.VMEM)
    hbm = pl.BlockSpec(memory_space=pl.ANY)
    tall = owned + halo
    turns = ITERS
    out, part = pl.pallas_call(
        functools.partial(kernel, n),
        out_shape=(
            jax.ShapeDtypeStruct((rows, owned), F32),
            jax.ShapeDtypeStruct((count, modes), F32),
        ),
        in_specs=[hbm, hbm, vmem, hbm] + [vmem] * 5,
        out_specs=(hbm, vmem),
        scratch_shapes=[
            pltpu.VMEM((nvar, count, owned), F32),
            pltpu.VMEM((nvar, nvar, count, owned), BF16),
            pltpu.VMEM((nvar, modes, owned), F32),
            pltpu.VMEM((3 * rows, 3 * rows), BF16),
            pltpu.VMEM((1, 128), F32),
            pltpu.VMEM((tall, nfaces), BF16),
            pltpu.VMEM((owned, nfaces), BF16),
            pltpu.VMEM((halo, nfaces), BF16),
            pltpu.VMEM((owned, owned), BF16),
            pltpu.VMEM((owned, owned), F8),
            pltpu.VMEM((owned, owned), BF16),
            pltpu.VMEM((owned, owned), F8),
            pltpu.VMEM((2 * halo, owned), BF16),
            pltpu.VMEM((2 * halo, owned), BF16),
            pltpu.VMEM((256, owned), BF16),
            pltpu.VMEM((owned, 2 * halo + 256), BF16),
            pltpu.VMEM((rows, owned), F32),
            pltpu.VMEM((rows, owned), F32),
            pltpu.VMEM((rows, owned), F32),
            pltpu.VMEM((2, 2 * rows, owned), BF16),
            pltpu.VMEM((2, 96, owned), F8),
            pltpu.VMEM((turns, n, count // 2, 128), F32),
            pltpu.VMEM((turns - 1, 2, rows, halo), F32),
            pltpu.VMEM((turns - 1, 2, rows, halo), F32),
            pltpu.SemaphoreType.DMA((3,)),
            pltpu.SemaphoreType.DMA((turns, n)),
            pltpu.SemaphoreType.DMA((turns, n)),
            pltpu.SemaphoreType.DMA((turns - 1, 2)),
            pltpu.SemaphoreType.DMA((turns - 1, 2)),
        ],
        compiler_params=pltpu.CompilerParams(
            collective_id=0, has_side_effects=True, vmem_limit_bytes=56 * 1024 * 1024
        ),
    )(
        jnp.transpose(adjoint_seed, (1, 0, 2)),
        inverse,
        jnp.transpose(flux_jacobians, (2, 3, 0, 1)),
        jnp.transpose(modal_shapes, (1, 0, 2)),
        modal_gain[None, :],
        face_cells,
        face_weights.reshape(nfaces // 128, 128),
        colours[None, :],
        send_cells,
    )
    out, part = pl.pallas_call(
        hand_over,
        out_shape=(
            jax.ShapeDtypeStruct((rows, owned), F32),
            jax.ShapeDtypeStruct((count, modes), F32),
        ),
        in_specs=[hbm, hbm],
        out_specs=(hbm, hbm),
        scratch_shapes=[
            pltpu.VMEM((rows, owned), F32),
            pltpu.VMEM((count, modes), F32),
            pltpu.SemaphoreType.DMA((2, 6)),
        ],
    )(out, part)
    return jnp.transpose(out.reshape(nvar, count, owned), (1, 0, 2)), part


def solution(mesh):
    return jax.shard_map(
        local,
        mesh=mesh,
        in_specs=(
            P("group", None, "cell"),
            P("group", None, None, "cell"),
            P(None, "group", None, None),
            P(None, None, "cell"),
            P("group"),
            P(None, "cell"),
            P("cell"),
            P("cell"),
            P(None, "cell"),
        ),
        out_specs=(P("group", None, "cell"), P("group", None)),
        check_vma=False,
    )
```

```python
import functools
import math

import jax
import jax.numpy as jnp
from jax import lax
from jax.experimental import pallas as pl
from jax.experimental.pallas import tpu as pltpu
from jax.sharding import PartitionSpec as P

ITERS = 4
FREQUENCY = 0.04
F32 = jnp.float32
BF16 = jnp.bfloat16
F8 = jnp.float8_e4m3fn
LIFT = 256.0
F8_MAX = 448.0
SPAN = 32.0
MODE_ROWS = 24
CANDIDATES = 64


def spectral_weights(count):
    return [FREQUENCY * 0.5 * (-1.0) ** d / math.tan(math.pi * d / count) for d in range(1, count)]


def bf16_factors(value):
    best_p = value.astype(BF16).astype(F32)
    best_q = jnp.ones_like(value)
    best = jnp.abs(value - best_p)
    for k in range(1, CANDIDATES):
        q = 1.0 + k / 128.0
        p = (value * (1.0 / q)).astype(BF16).astype(F32)
        miss = jnp.abs(value - p * q)
        better = miss < best
        best = jnp.where(better, miss, best)
        best_p = jnp.where(better, p, best_p)
        best_q = jnp.where(better, q, best_q)
    return best_p.astype(BF16), best_q.astype(BF16)


def split(value):
    high = value.astype(BF16)
    return high, (value - high.astype(F32)).astype(BF16)


def split_f8(value):
    high = value.astype(BF16)
    low = (value - high.astype(F32)) * LIFT
    return high, jnp.clip(low, -F8_MAX, F8_MAX).astype(F8)


def mm(left, right):
    return jnp.dot(left, right, preferred_element_type=F32)


def mm_nt(left, right):
    return lax.dot_general(left, right, (((1,), (1,)), ((), ())), preferred_element_type=F32)


def kernel(
    n,
    seed_hbm,
    inv_hbm,
    flux_ref,
    shapes_hbm,
    gain_ref,
    faces_ref,
    g_ref,
    col_ref,
    send_ref,
    out_hbm,
    part_ref,
    seed_ref,
    inv_ref,
    shapes_ref,
    w_ref,
    gain_pad,
    left_hot,
    right_hot,
    upper_hot,
    index_rows,
    value_rows,
    m_high,
    m_low,
    t_high,
    t_low,
    mg_high,
    mg_low,
    p_ref,
    sel_ref,
    x_ref,
    z_ref,
    base_ref,
    ab_ref,
    ab_low,
    q_all,
    ghost_out,
    ghost_in,
    in_sem,
    q_send,
    q_recv,
    g_send,
    g_recv,
):
    nvar, count, owned = seed_ref.shape
    modes = shapes_ref.shape[1]
    rows = count * nvar
    halo = send_ref.shape[1]
    nfaces = faces_ref.shape[1]
    me = lax.axis_index("cell")
    lower, upper = lax.rem(me + n - 1, n), lax.rem(me + 1, n)
    peers = partners(me, n)
    loads = [
        pltpu.make_async_copy(src, dst, in_sem.at[k])
        for k, (src, dst) in enumerate(
            [(seed_hbm, seed_ref), (shapes_hbm, shapes_ref), (inv_hbm, inv_ref)]
        )
    ]
    for load in loads:
        load.start()

    barrier = pltpu.get_barrier_semaphore()
    for d in range(1, n):
        pl.semaphore_signal(barrier, inc=1, device_id={"cell": peers[d]}, device_id_type=pl.DeviceIdType.MESH)

    left = faces_ref[0:1, :].astype(jnp.int16)
    right = faces_ref[1:2, :].astype(jnp.int16)
    p_tile, q_tile = bf16_factors(g_ref[...])
    p_tile, q_tile = p_tile.astype(F32), q_tile.astype(F32)
    p_row = jnp.concatenate([p_tile[k : k + 1, :] for k in range(nfaces // 128)], axis=1).astype(BF16)
    q_row = jnp.concatenate([q_tile[k : k + 1, :] for k in range(nfaces // 128)], axis=1).astype(BF16)
    step = 128
    tall = owned + halo

    for k, row in enumerate((left, right)):
        index_rows[k] = jnp.broadcast_to(row, (16, nfaces))
    for k, row in enumerate((p_row, q_row)):
        value_rows[k] = jnp.broadcast_to(row, (16, nfaces))
    sixteen = lax.broadcasted_iota(jnp.int32, (16, 128), 0)

    def hot(side, start, size):
        near = index_rows[side]
        value = value_rows[side]
        zero = jnp.zeros((16, nfaces), BF16)
        strips = []
        for k in range(size // 16):
            line = (sixteen + (start + 16 * k)).astype(jnp.int16)
            strips.append(jnp.where(near == jnp.concatenate([line] * (nfaces // 128), axis=1), value, zero))
        return jnp.concatenate(strips, axis=0)

    @pl.loop(0, tall // step)
    def _(t):
        at = pl.multiple_of(t * step, step)
        left_hot[pl.ds(at, step), :] = hot(0, at, step)

    upper_hot[...] = hot(1, owned + halo, halo)
    wide = 256
    tall_step = owned // 2

    send_row = jnp.concatenate([send_ref[0:1, :], send_ref[1:2, :]], axis=1)
    for load in loads:
        load.wait()

    @pl.loop(0, owned // wide)
    def _(t):
        at = pl.multiple_of(t * wide, wide)
        here = pl.ds(at, wide)
        sel_ref[here, 0 : 2 * halo] = jnp.where(
            send_row - at == lax.broadcasted_iota(jnp.int32, (wide, 2 * halo), 0), 1.0, 0.0
        ).astype(BF16)
        pad = jnp.zeros((MODE_ROWS - modes, wide), F32)
        lines = []
        for v in range(nvar):
            lines += [shapes_ref[v, :, here], pad]
            z_ref[v * count : (v + 1) * count, here] = seed_ref[v, :, here]
            base_ref[v * count : (v + 1) * count, here] = seed_ref[v, :, here]
        lines.append(jnp.zeros((128 - nvar * MODE_ROWS, wide), F32))
        high, low = split(jnp.concatenate(lines, axis=0))
        p_ref[0:128, here] = high
        p_ref[128:256, here] = low
        sel_ref[here, 2 * halo : 2 * halo + 128] = high.astype(F32).T.astype(BF16)
        sel_ref[here, 2 * halo + 128 :] = low.astype(F32).T.astype(BF16)
        right_now = hot(1, at, wide)
        right_hot[pl.ds(at, wide), :] = right_now
        for part in range(owned // tall_step):
            r0 = part * tall_step
            block = mm_nt(left_hot[r0 : r0 + tall_step, :], right_now)
            high, low = split_f8(block)
            m_high[r0 : r0 + tall_step, pl.ds(at, wide)] = high
            m_low[r0 : r0 + tall_step, pl.ds(at, wide)] = low
            high, low = split_f8(block.T)
            t_high[pl.ds(at, wide), r0 : r0 + tall_step] = high
            t_low[pl.ds(at, wide), r0 : r0 + tall_step] = low

    def build_ghost_matrix():
        @pl.loop(0, owned // wide)
        def _(t):
            at = pl.multiple_of(t * wide, wide)
            high, low = split(mm_nt(left_hot[owned:tall, :], right_hot[pl.ds(at, wide), :]))
            mg_high[0:halo, pl.ds(at, wide)] = high
            mg_low[0:halo, pl.ds(at, wide)] = low
            high, low = split(mm_nt(upper_hot[...], left_hot[pl.ds(at, wide), :]))
            mg_high[halo:, pl.ds(at, wide)] = high
            mg_low[halo:, pl.ds(at, wide)] = low

    eye_line = lax.broadcasted_iota(jnp.int32, (count, rows), 0)
    eye_lane = lax.broadcasted_iota(jnp.int32, (count, rows), 1)
    eye = lax.rem(eye_lane, count) == eye_line
    blocks = []
    for side in range(2):
        for w in range(nvar):
            row = jnp.concatenate([flux_ref[v, w][side : side + 1, :] for v in range(nvar)], axis=1)
            blocks.append(jnp.where(eye, jnp.broadcast_to(row, (count, rows)), 0.0))
    line = lax.broadcasted_iota(jnp.int32, (rows, rows), 0)
    lane = lax.broadcasted_iota(jnp.int32, (rows, rows), 1)
    apart = lax.rem(lane, count) - lax.rem(line, count)
    spectral = jnp.zeros((rows, rows), F32)
    for d, weight in enumerate(spectral_weights(count), 1):
        spectral = jnp.where(apart == d, weight, jnp.where(apart == -d, -weight, spectral))
    spectral = jnp.where(lax.div(lane, count) == lax.div(line, count), spectral, 0.0)
    w_high, w_low = split(jnp.concatenate(blocks + [spectral], axis=0))
    lane = lax.broadcasted_iota(jnp.int32, (rows, 3 * rows), 1)
    line = lax.broadcasted_iota(jnp.int32, (rows, 3 * rows), 0)
    first = jnp.where((lane == line) | (lane == line + rows), 1.0, 0.0).astype(BF16)
    last = jnp.where(lane == line + 2 * rows, 1.0, 0.0).astype(BF16)
    w_ref[...] = (mm(w_high, first) + mm(w_low, last)).astype(BF16)
    gain_pad[...] = jnp.zeros((1, 128), F32)
    gain_pad[:, 0:modes] = gain_ref[...]
    colours = col_ref[...]

    def update(colour):
        mask = colours == colour
        for w in range(nvar):
            spot = slice(w * count, (w + 1) * count)
            total = inv_ref[0, w].astype(F32) * z_ref[0:count, :]
            for v in range(1, nvar):
                total = total + inv_ref[v, w].astype(F32) * z_ref[v * count : (v + 1) * count, :]
            x_ref[spot, :] = jnp.where(mask, total, x_ref[spot, :])

    def coupling():
        value = x_ref[...]
        top = jnp.max(jnp.abs(value), axis=0, keepdims=True)
        top = jnp.maximum(jnp.max(top, axis=1, keepdims=True), 1e-30)
        scale = SPAN / top
        high, low = split(value)
        both = mm(w_ref[...], jnp.concatenate([high, low, high], axis=0))
        for side in range(2):
            part = both[side * rows : (side + 1) * rows]
            high, low = split(part)
            ab_ref[side, 0:rows, :] = high
            ab_ref[side, rows:, :] = low
            rough = jnp.concatenate([part * scale, jnp.zeros((96 - rows, owned), F32)], axis=0)
            ab_low[side] = rough.astype(F8)
        one = mm(ab_ref[0], m_high[...]) + mm(ab_ref[1], t_high[...])
        two = mm(ab_low[0], m_low[...]) + mm(ab_low[1], t_low[...])
        z_ref[...] = both[2 * rows :] + (one[:rows] + one[rows:] + two[:rows] * (top * (1.0 / (SPAN * LIFT))))

    def modal_copies(turn):
        return [
            pltpu.make_async_remote_copy(
                src_ref=q_all.at[turn, me],
                dst_ref=q_all.at[turn, me],
                send_sem=q_send.at[turn],
                recv_sem=q_recv.at[turn],
                device_id={"cell": peers[d]},
                device_id_type=pl.DeviceIdType.MESH,
            )
            for d in range(n - 1, 0, -1)
        ]

    def wait_modal(turn):
        every = q_all.at[turn, pl.ds(0, n - 1)]
        pltpu.make_async_copy(every, every, q_send.at[turn]).wait()
        pltpu.make_async_copy(every, every, q_recv.at[turn]).wait()

    def ghost_copies(turn):
        return [
            pltpu.make_async_remote_copy(
                src_ref=ghost_out.at[turn, way],
                dst_ref=ghost_in.at[turn, 1 - way],
                send_sem=g_send.at[turn, way],
                recv_sem=g_recv.at[turn, way],
                device_id={"cell": lower if way == 0 else upper},
                device_id_type=pl.DeviceIdType.MESH,
            )
            for way in range(2)
        ]

    def start_exchange(turn):
        high, low = split(x_ref[...])
        every = mm(jnp.concatenate([high, low], axis=0), sel_ref[...])
        every = every[:rows] + every[rows:]
        gram = every[:, 2 * halo : 2 * halo + 128] + every[:, 2 * halo + 128 :]
        part = gram[0:count, 0:MODE_ROWS]
        for v in range(1, nvar):
            part = part + gram[v * count : (v + 1) * count, v * MODE_ROWS : (v + 1) * MODE_ROWS]
        half = count // 2
        q_all[turn, me] = jnp.concatenate(
            [part[:half], part[half:], jnp.zeros((half, 128 - 2 * MODE_ROWS), F32)], axis=1
        )

        @pl.when(turn == 0)
        def _():
            pl.semaphore_wait(barrier, n - 1)

        for copy in modal_copies(turn):
            copy.start()

        @pl.when(turn < ITERS - 1)
        def _():
            ghost_out[turn, 0] = every[:, :halo]
            ghost_out[turn, 1] = every[:, halo : 2 * halo]
            for copy in ghost_copies(turn):
                copy.start()

    def modal_sum(turn):
        total = q_all[turn, 0]
        for d in range(1, n):
            total = total + q_all[turn, d]
        return jnp.concatenate([total[:, :MODE_ROWS], total[:, MODE_ROWS : 2 * MODE_ROWS]], axis=0)

    x_ref[...] = jnp.zeros((rows, owned), F32)
    @pl.loop(0, ITERS)
    def _(sweep):
        @pl.when(sweep > 0)
        def _():
            coupling()

            @pl.when(sweep == 1)
            def _():
                build_ghost_matrix()

            for copy in ghost_copies(sweep - 1):
                copy.wait()
            wait_modal(sweep - 1)
            low_part = ghost_in[sweep - 1, 0]
            up_part = ghost_in[sweep - 1, 1]
            high, low = split(jnp.concatenate([low_part, up_part], axis=1))
            both = mm(w_ref[0 : 2 * rows, :], jnp.concatenate([high, low, high], axis=0))
            ghost_ab = jnp.concatenate([both[:rows, :halo], both[rows:, halo:]], axis=1)
            ghost_high, ghost_low = split(ghost_ab)
            lam = modal_sum(sweep - 1) * gain_pad[:, :MODE_ROWS]
            lam = jnp.concatenate([lam] * nvar + [jnp.zeros((count, 128 - nvar * MODE_ROWS), F32)], axis=1)
            lam = jnp.concatenate([lam] * nvar, axis=0)
            lane = lax.broadcasted_iota(jnp.int32, (rows, 128), 1)
            line = lax.broadcasted_iota(jnp.int32, (rows, 128), 0)
            lam = jnp.where(lax.div(lane, MODE_ROWS) == lax.div(line, count), -lam, 0.0)
            lam_high, lam_low = split(lam)
            term = mm(jnp.concatenate([ghost_high, ghost_low], axis=0), mg_high[...]) + mm(
                jnp.concatenate([lam_high, lam_low], axis=0), p_ref[0:128, :]
            )
            rest = mm(ghost_high, mg_low[...]) + mm(lam_high, p_ref[128:256, :])
            term = term[:rows] + term[rows:] + rest
            for v in range(nvar):
                spot = slice(v * count, (v + 1) * count)
                base = seed_ref[v] - term[spot]
                base_ref[spot, :] = base
                z_ref[spot, :] = base - z_ref[spot, :]

        update(0)
        coupling()
        z_ref[...] = base_ref[...] - z_ref[...]
        update(1)
        start_exchange(sweep)

    store = pltpu.make_async_copy(x_ref, out_hbm, in_sem.at[0])
    store.start()
    wait_modal(ITERS - 1)
    part_ref[...] = modal_sum(ITERS - 1)[:, :modes]
    store.wait()


def partners(me, n):
    if n & (n - 1):
        return [lax.rem(me + d, n) for d in range(n)]
    places = []
    for d in range(n):
        place = me
        bit = 1
        while bit < n:
            if d & bit:
                place = place + bit - 2 * bit * lax.rem(lax.div(me, bit), 2)
            bit *= 2
        places.append(place)
    return places


def hand_over(out_ref, part_ref, out_final, part_final, stage, small, sem):
    pieces = 5
    size = out_ref.shape[0] // pieces
    spots = [pl.ds(k * size, size) for k in range(pieces)]
    ins = [pltpu.make_async_copy(out_ref.at[s], stage.at[s], sem.at[0, k]) for k, s in enumerate(spots)]
    outs = [pltpu.make_async_copy(stage.at[s], out_final.at[s], sem.at[1, k]) for k, s in enumerate(spots)]
    ins.append(pltpu.make_async_copy(part_ref, small, sem.at[0, pieces]))
    outs.append(pltpu.make_async_copy(small, part_final, sem.at[1, pieces]))
    for copy in ins:
        copy.start()
    for first, second in zip(ins, outs):
        first.wait()
        second.start()
    for copy in outs:
        copy.wait()


def local(
    adjoint_seed,
    inv_blocks,
    flux_jacobians,
    modal_shapes,
    modal_gain,
    face_cells,
    face_weights,
    colours,
    send_cells,
):
    n = lax.axis_size("cell")
    count, nvar, owned = adjoint_seed.shape
    modes = modal_shapes.shape[0]
    rows = count * nvar
    halo = send_cells.shape[1]
    nfaces = face_weights.shape[0]
    inverse = jnp.transpose(inv_blocks, (1, 2, 0, 3))
    vmem = pl.BlockSpec(memory_space=pltpu.VMEM)
    hbm = pl.BlockSpec(memory_space=pl.ANY)
    tall = owned + halo
    turns = ITERS
    out, part = pl.pallas_call(
        functools.partial(kernel, n),
        out_shape=(
            jax.ShapeDtypeStruct((rows, owned), F32),
            jax.ShapeDtypeStruct((count, modes), F32),
        ),
        in_specs=[hbm, hbm, vmem, hbm] + [vmem] * 5,
        out_specs=(hbm, vmem),
        scratch_shapes=[
            pltpu.VMEM((nvar, count, owned), F32),
            pltpu.VMEM((nvar, nvar, count, owned), BF16),
            pltpu.VMEM((nvar, modes, owned), F32),
            pltpu.VMEM((3 * rows, 3 * rows), BF16),
            pltpu.VMEM((1, 128), F32),
            pltpu.VMEM((tall, nfaces), BF16),
            pltpu.VMEM((owned, nfaces), BF16),
            pltpu.VMEM((halo, nfaces), BF16),
            pltpu.VMEM((2, 16, nfaces), jnp.int16),
            pltpu.VMEM((2, 16, nfaces), BF16),
            pltpu.VMEM((owned, owned), BF16),
            pltpu.VMEM((owned, owned), F8),
            pltpu.VMEM((owned, owned), BF16),
            pltpu.VMEM((owned, owned), F8),
            pltpu.VMEM((2 * halo, owned), BF16),
            pltpu.VMEM((2 * halo, owned), BF16),
            pltpu.VMEM((256, owned), BF16),
            pltpu.VMEM((owned, 2 * halo + 256), BF16),
            pltpu.VMEM((rows, owned), F32),
            pltpu.VMEM((rows, owned), F32),
            pltpu.VMEM((rows, owned), F32),
            pltpu.VMEM((2, 2 * rows, owned), BF16),
            pltpu.VMEM((2, 96, owned), F8),
            pltpu.VMEM((turns, n, count // 2, 128), F32),
            pltpu.VMEM((turns - 1, 2, rows, halo), F32),
            pltpu.VMEM((turns - 1, 2, rows, halo), F32),
            pltpu.SemaphoreType.DMA((3,)),
            pltpu.SemaphoreType.DMA((turns,)),
            pltpu.SemaphoreType.DMA((turns,)),
            pltpu.SemaphoreType.DMA((turns - 1, 2)),
            pltpu.SemaphoreType.DMA((turns - 1, 2)),
        ],
        compiler_params=pltpu.CompilerParams(
            collective_id=0, has_side_effects=True, vmem_limit_bytes=56 * 1024 * 1024
        ),
    )(
        jnp.transpose(adjoint_seed, (1, 0, 2)),
        inverse,
        jnp.transpose(flux_jacobians, (2, 3, 0, 1)),
        jnp.transpose(modal_shapes, (1, 0, 2)),
        modal_gain[None, :],
        face_cells,
        face_weights.reshape(nfaces // 128, 128),
        colours[None, :],
        send_cells,
    )
    out, part = pl.pallas_call(
        hand_over,
        out_shape=(
            jax.ShapeDtypeStruct((rows, owned), F32),
            jax.ShapeDtypeStruct((count, modes), F32),
        ),
        in_specs=[hbm, hbm],
        out_specs=(hbm, hbm),
        scratch_shapes=[
            pltpu.VMEM((rows, owned), F32),
            pltpu.VMEM((count, modes), F32),
            pltpu.SemaphoreType.DMA((2, 6)),
        ],
    )(out, part)
    return jnp.transpose(out.reshape(nvar, count, owned), (1, 0, 2)), part


def solution(mesh):
    return jax.shard_map(
        local,
        mesh=mesh,
        in_specs=(
            P("group", None, "cell"),
            P("group", None, None, "cell"),
            P(None, "group", None, None),
            P(None, None, "cell"),
            P("group"),
            P(None, "cell"),
            P("cell"),
            P("cell"),
            P(None, "cell"),
        ),
        out_specs=(P("group", None, "cell"), P("group", None)),
        check_vma=False,
    )
```

```python
import functools
import math

import jax
import jax.numpy as jnp
from jax import lax
from jax.experimental import pallas as pl
from jax.experimental.pallas import tpu as pltpu
from jax.sharding import PartitionSpec as P

ITERS = 4
FREQUENCY = 0.04
F32 = jnp.float32
BF16 = jnp.bfloat16
F8 = jnp.float8_e4m3fn
LIFT = 256.0
F8_MAX = 448.0
SPAN = 32.0
MODE_ROWS = 24
CANDIDATES = 64


def spectral_weights(count):
    return [FREQUENCY * 0.5 * (-1.0) ** d / math.tan(math.pi * d / count) for d in range(1, count)]


def bf16_factors(value):
    best_p = value.astype(BF16).astype(F32)
    best_q = jnp.ones_like(value)
    best = jnp.abs(value - best_p)
    for k in range(1, CANDIDATES):
        q = 1.0 + k / 128.0
        p = (value * (1.0 / q)).astype(BF16).astype(F32)
        miss = jnp.abs(value - p * q)
        better = miss < best
        best = jnp.where(better, miss, best)
        best_p = jnp.where(better, p, best_p)
        best_q = jnp.where(better, q, best_q)
    return best_p.astype(BF16), best_q.astype(BF16)


def split(value):
    high = value.astype(BF16)
    return high, (value - high.astype(F32)).astype(BF16)


def split_f8(value):
    high = value.astype(BF16)
    low = (value - high.astype(F32)) * LIFT
    return high, jnp.clip(low, -F8_MAX, F8_MAX).astype(F8)


def mm(left, right):
    return jnp.dot(left, right, preferred_element_type=F32)


def mm_nt(left, right):
    return lax.dot_general(left, right, (((1,), (1,)), ((), ())), preferred_element_type=F32)


def kernel(
    n,
    seed_hbm,
    inv_hbm,
    flux_ref,
    shapes_hbm,
    gain_ref,
    faces_ref,
    g_ref,
    col_ref,
    send_ref,
    out_hbm,
    part_ref,
    seed_ref,
    inv_ref,
    shapes_ref,
    w_ref,
    gain_pad,
    left_hot,
    upper_hot,
    block_a,
    block_b,
    index_rows,
    value_rows,
    m_high,
    m_low,
    t_high,
    t_low,
    mg_high,
    mg_low,
    p_ref,
    sel_ref,
    x_ref,
    z_ref,
    base_ref,
    ab_ref,
    ab_low,
    q_all,
    ghost_out,
    ghost_in,
    in_sem,
    q_send,
    q_recv,
    g_send,
    g_recv,
):
    nvar, count, owned = seed_ref.shape
    modes = shapes_ref.shape[1]
    rows = count * nvar
    halo = send_ref.shape[1]
    nfaces = faces_ref.shape[1]
    me = lax.axis_index("cell")
    lower, upper = lax.rem(me + n - 1, n), lax.rem(me + 1, n)
    peers = partners(me, n)
    loads = [
        pltpu.make_async_copy(src, dst, in_sem.at[k])
        for k, (src, dst) in enumerate(
            [(seed_hbm, seed_ref), (shapes_hbm, shapes_ref), (inv_hbm, inv_ref)]
        )
    ]
    for load in loads:
        load.start()

    barrier = pltpu.get_barrier_semaphore()
    for d in range(1, n):
        pl.semaphore_signal(barrier, inc=1, device_id={"cell": peers[d]}, device_id_type=pl.DeviceIdType.MESH)

    left = faces_ref[0:1, :].astype(jnp.int16)
    right = faces_ref[1:2, :].astype(jnp.int16)
    p_tile, q_tile = bf16_factors(g_ref[...])
    p_tile, q_tile = p_tile.astype(F32), q_tile.astype(F32)
    p_row = jnp.concatenate([p_tile[k : k + 1, :] for k in range(nfaces // 128)], axis=1).astype(BF16)
    q_row = jnp.concatenate([q_tile[k : k + 1, :] for k in range(nfaces // 128)], axis=1).astype(BF16)
    step = 128
    wide = 256
    tall_step = owned // 2
    tall = owned + halo

    for k, row in enumerate((left, right)):
        index_rows[k] = jnp.broadcast_to(row, (16, nfaces))
    for k, row in enumerate((p_row, q_row)):
        value_rows[k] = jnp.broadcast_to(row, (16, nfaces))
    sixteen = lax.broadcasted_iota(jnp.int32, (16, 128), 0)

    def hot(side, start, size):
        near = index_rows[side]
        value = value_rows[side]
        zero = jnp.zeros((16, nfaces), BF16)
        strips = []
        for k in range(size // 16):
            line = (sixteen + (start + 16 * k)).astype(jnp.int16)
            strips.append(jnp.where(near == jnp.concatenate([line] * (nfaces // 128), axis=1), value, zero))
        return jnp.concatenate(strips, axis=0)

    blocks_ref = (block_a, block_b)

    def split_block(at, slot):
        here = pl.ds(at, wide)
        for part in range(owned // tall_step):
            r0 = part * tall_step
            block = blocks_ref[slot][r0 : r0 + tall_step, :]
            high, low = split_f8(block)
            m_high[r0 : r0 + tall_step, here] = high
            m_low[r0 : r0 + tall_step, here] = low
            high, low = split_f8(block.T)
            t_high[here, r0 : r0 + tall_step] = high
            t_low[here, r0 : r0 + tall_step] = low
        high, low = split(blocks_ref[slot][owned:tall, :])
        mg_high[0:halo, here] = high
        mg_low[0:halo, here] = low

    @pl.loop(0, tall // step)
    def _(t):
        at = pl.multiple_of(t * step, step)
        left_hot[pl.ds(at, step), :] = hot(0, at, step)

    upper_hot[...] = hot(1, owned + halo, halo)

    send_row = jnp.concatenate([send_ref[0:1, :], send_ref[1:2, :]], axis=1)
    for load in loads:
        load.wait()

    def build_tile(t, slot):
        at = pl.multiple_of(t * wide, wide)
        here = pl.ds(at, wide)
        sel_ref[here, 0 : 2 * halo] = jnp.where(
            send_row - at == lax.broadcasted_iota(jnp.int32, (wide, 2 * halo), 0), 1.0, 0.0
        ).astype(BF16)
        pad = jnp.zeros((MODE_ROWS - modes, wide), F32)
        lines = []
        for v in range(nvar):
            lines += [shapes_ref[v, :, here], pad]
            z_ref[v * count : (v + 1) * count, here] = seed_ref[v, :, here]
            base_ref[v * count : (v + 1) * count, here] = seed_ref[v, :, here]
        lines.append(jnp.zeros((128 - nvar * MODE_ROWS, wide), F32))
        high, low = split(jnp.concatenate(lines, axis=0))
        p_ref[0:128, here] = high
        p_ref[128:256, here] = low
        sel_ref[here, 2 * halo : 2 * halo + 128] = high.astype(F32).T.astype(BF16)
        sel_ref[here, 2 * halo + 128 :] = low.astype(F32).T.astype(BF16)
        right_now = hot(1, at, wide)
        earlier = lax.rem(t + owned // wide - 1, owned // wide)
        split_block(pl.multiple_of(earlier * wide, wide), 1 - slot)
        for part in range(2):
            r0 = part * (tall // 2)
            blocks_ref[slot][r0 : r0 + tall // 2, :] = mm_nt(left_hot[r0 : r0 + tall // 2, :], right_now)

    @pl.loop(0, owned // (2 * wide))
    def _(t):
        build_tile(2 * t, 0)
        build_tile(2 * t + 1, 1)

    split_block(owned - wide, (owned // wide - 1) % 2)

    def build_ghost_matrix():
        @pl.loop(0, owned // wide)
        def _(t):
            at = pl.multiple_of(t * wide, wide)
            high, low = split(mm_nt(upper_hot[...], left_hot[pl.ds(at, wide), :]))
            mg_high[halo:, pl.ds(at, wide)] = high
            mg_low[halo:, pl.ds(at, wide)] = low

    eye_line = lax.broadcasted_iota(jnp.int32, (count, rows), 0)
    eye_lane = lax.broadcasted_iota(jnp.int32, (count, rows), 1)
    eye = lax.rem(eye_lane, count) == eye_line
    blocks = []
    for side in range(2):
        for w in range(nvar):
            row = jnp.concatenate([flux_ref[v, w][side : side + 1, :] for v in range(nvar)], axis=1)
            blocks.append(jnp.where(eye, jnp.broadcast_to(row, (count, rows)), 0.0))
    line = lax.broadcasted_iota(jnp.int32, (rows, rows), 0)
    lane = lax.broadcasted_iota(jnp.int32, (rows, rows), 1)
    apart = lax.rem(lane, count) - lax.rem(line, count)
    spectral = jnp.zeros((rows, rows), F32)
    for d, weight in enumerate(spectral_weights(count), 1):
        spectral = jnp.where(apart == d, weight, jnp.where(apart == -d, -weight, spectral))
    spectral = jnp.where(lax.div(lane, count) == lax.div(line, count), spectral, 0.0)
    w_high, w_low = split(jnp.concatenate(blocks + [spectral], axis=0))
    lane = lax.broadcasted_iota(jnp.int32, (rows, 3 * rows), 1)
    line = lax.broadcasted_iota(jnp.int32, (rows, 3 * rows), 0)
    first = jnp.where((lane == line) | (lane == line + rows), 1.0, 0.0).astype(BF16)
    last = jnp.where(lane == line + 2 * rows, 1.0, 0.0).astype(BF16)
    w_ref[...] = (mm(w_high, first) + mm(w_low, last)).astype(BF16)
    gain_pad[...] = jnp.zeros((1, 128), F32)
    gain_pad[:, 0:modes] = gain_ref[...]
    colours = col_ref[...]

    def update(colour):
        mask = colours == colour
        for w in range(nvar):
            spot = slice(w * count, (w + 1) * count)
            total = inv_ref[0, w].astype(F32) * z_ref[0:count, :]
            for v in range(1, nvar):
                total = total + inv_ref[v, w].astype(F32) * z_ref[v * count : (v + 1) * count, :]
            x_ref[spot, :] = jnp.where(mask, total, x_ref[spot, :])

    def coupling():
        value = x_ref[...]
        top = jnp.max(jnp.abs(value), axis=0, keepdims=True)
        top = jnp.maximum(jnp.max(top, axis=1, keepdims=True), 1e-30)
        scale = SPAN / top
        high, low = split(value)
        both = mm(w_ref[...], jnp.concatenate([high, low, high], axis=0))
        for side in range(2):
            part = both[side * rows : (side + 1) * rows]
            high, low = split(part)
            ab_ref[side, 0:rows, :] = high
            ab_ref[side, rows:, :] = low
            rough = jnp.concatenate([part * scale, jnp.zeros((96 - rows, owned), F32)], axis=0)
            ab_low[side] = rough.astype(F8)
        one = mm(ab_ref[0], m_high[...]) + mm(ab_ref[1], t_high[...])
        two = mm(ab_low[0], m_low[...]) + mm(ab_low[1], t_low[...])
        z_ref[...] = both[2 * rows :] + (one[:rows] + one[rows:] + two[:rows] * (top * (1.0 / (SPAN * LIFT))))

    def modal_copies(turn):
        return [
            pltpu.make_async_remote_copy(
                src_ref=q_all.at[turn, me],
                dst_ref=q_all.at[turn, me],
                send_sem=q_send.at[turn],
                recv_sem=q_recv.at[turn],
                device_id={"cell": peers[d]},
                device_id_type=pl.DeviceIdType.MESH,
            )
            for d in range(n - 1, 0, -1)
        ]

    def wait_modal(turn):
        every = q_all.at[turn, pl.ds(0, n - 1)]
        pltpu.make_async_copy(every, every, q_send.at[turn]).wait()
        pltpu.make_async_copy(every, every, q_recv.at[turn]).wait()

    def ghost_copies(turn):
        return [
            pltpu.make_async_remote_copy(
                src_ref=ghost_out.at[turn, way],
                dst_ref=ghost_in.at[turn, 1 - way],
                send_sem=g_send.at[turn, way],
                recv_sem=g_recv.at[turn, way],
                device_id={"cell": lower if way == 0 else upper},
                device_id_type=pl.DeviceIdType.MESH,
            )
            for way in range(2)
        ]

    def start_exchange(turn):
        high, low = split(x_ref[...])
        every = mm(jnp.concatenate([high, low], axis=0), sel_ref[...])
        every = every[:rows] + every[rows:]
        gram = every[:, 2 * halo : 2 * halo + 128] + every[:, 2 * halo + 128 :]
        part = gram[0:count, 0:MODE_ROWS]
        for v in range(1, nvar):
            part = part + gram[v * count : (v + 1) * count, v * MODE_ROWS : (v + 1) * MODE_ROWS]
        half = count // 2
        q_all[turn, me] = jnp.concatenate(
            [part[:half], part[half:], jnp.zeros((half, 128 - 2 * MODE_ROWS), F32)], axis=1
        )

        @pl.when(turn == 0)
        def _():
            pl.semaphore_wait(barrier, n - 1)

        for copy in modal_copies(turn):
            copy.start()

        @pl.when(turn < ITERS - 1)
        def _():
            ghost_out[turn, 0] = every[:, :halo]
            ghost_out[turn, 1] = every[:, halo : 2 * halo]
            for copy in ghost_copies(turn):
                copy.start()

    def modal_sum(turn):
        total = q_all[turn, 0]
        for d in range(1, n):
            total = total + q_all[turn, d]
        return jnp.concatenate([total[:, :MODE_ROWS], total[:, MODE_ROWS : 2 * MODE_ROWS]], axis=0)

    x_ref[...] = jnp.zeros((rows, owned), F32)
    @pl.loop(0, ITERS)
    def _(sweep):
        @pl.when(sweep > 0)
        def _():
            coupling()

            @pl.when(sweep == 1)
            def _():
                build_ghost_matrix()

            for copy in ghost_copies(sweep - 1):
                copy.wait()
            wait_modal(sweep - 1)
            low_part = ghost_in[sweep - 1, 0]
            up_part = ghost_in[sweep - 1, 1]
            high, low = split(jnp.concatenate([low_part, up_part], axis=1))
            both = mm(w_ref[0 : 2 * rows, :], jnp.concatenate([high, low, high], axis=0))
            ghost_ab = jnp.concatenate([both[:rows, :halo], both[rows:, halo:]], axis=1)
            ghost_high, ghost_low = split(ghost_ab)
            lam = modal_sum(sweep - 1) * gain_pad[:, :MODE_ROWS]
            lam = jnp.concatenate([lam] * nvar + [jnp.zeros((count, 128 - nvar * MODE_ROWS), F32)], axis=1)
            lam = jnp.concatenate([lam] * nvar, axis=0)
            lane = lax.broadcasted_iota(jnp.int32, (rows, 128), 1)
            line = lax.broadcasted_iota(jnp.int32, (rows, 128), 0)
            lam = jnp.where(lax.div(lane, MODE_ROWS) == lax.div(line, count), -lam, 0.0)
            lam_high, lam_low = split(lam)
            term = mm(jnp.concatenate([ghost_high, ghost_low], axis=0), mg_high[...]) + mm(
                jnp.concatenate([lam_high, lam_low], axis=0), p_ref[0:128, :]
            )
            rest = mm(ghost_high, mg_low[...]) + mm(lam_high, p_ref[128:256, :])
            term = term[:rows] + term[rows:] + rest
            for v in range(nvar):
                spot = slice(v * count, (v + 1) * count)
                base = seed_ref[v] - term[spot]
                base_ref[spot, :] = base
                z_ref[spot, :] = base - z_ref[spot, :]

        update(0)
        coupling()
        z_ref[...] = base_ref[...] - z_ref[...]
        update(1)
        start_exchange(sweep)

    out_hbm[...] = x_ref[...]
    wait_modal(ITERS - 1)
    part_ref[...] = modal_sum(ITERS - 1)[:, :modes]


def partners(me, n):
    if n & (n - 1):
        return [lax.rem(me + d, n) for d in range(n)]
    places = []
    for d in range(n):
        place = me
        bit = 1
        while bit < n:
            if d & bit:
                place = place + bit - 2 * bit * lax.rem(lax.div(me, bit), 2)
            bit *= 2
        places.append(place)
    return places


def hand_over(out_ref, part_ref, out_final, part_final, sem):
    first = pltpu.make_async_copy(out_ref, out_final, sem.at[0])
    second = pltpu.make_async_copy(part_ref, part_final, sem.at[1])
    first.start()
    second.start()
    first.wait()
    second.wait()


def local(
    adjoint_seed,
    inv_blocks,
    flux_jacobians,
    modal_shapes,
    modal_gain,
    face_cells,
    face_weights,
    colours,
    send_cells,
):
    n = lax.axis_size("cell")
    count, nvar, owned = adjoint_seed.shape
    modes = modal_shapes.shape[0]
    rows = count * nvar
    halo = send_cells.shape[1]
    nfaces = face_weights.shape[0]
    inverse = jnp.transpose(inv_blocks, (1, 2, 0, 3))
    vmem = pl.BlockSpec(memory_space=pltpu.VMEM)
    hbm = pl.BlockSpec(memory_space=pl.ANY)
    tall = owned + halo
    turns = ITERS
    out, part = pl.pallas_call(
        functools.partial(kernel, n),
        out_shape=(
            pltpu.VMEM((rows, owned), F32),
            pltpu.VMEM((count, modes), F32),
        ),
        in_specs=[hbm, hbm, vmem, hbm] + [vmem] * 5,
        out_specs=(vmem, vmem),
        scratch_shapes=[
            pltpu.VMEM((nvar, count, owned), F32),
            pltpu.VMEM((nvar, nvar, count, owned), BF16),
            pltpu.VMEM((nvar, modes, owned), F32),
            pltpu.VMEM((3 * rows, 3 * rows), BF16),
            pltpu.VMEM((1, 128), F32),
            pltpu.VMEM((tall, nfaces), BF16),
            pltpu.VMEM((halo, nfaces), BF16),
            pltpu.VMEM((tall, 256), F32),
            pltpu.VMEM((tall, 256), F32),
            pltpu.VMEM((2, 16, nfaces), jnp.int16),
            pltpu.VMEM((2, 16, nfaces), BF16),
            pltpu.VMEM((owned, owned), BF16),
            pltpu.VMEM((owned, owned), F8),
            pltpu.VMEM((owned, owned), BF16),
            pltpu.VMEM((owned, owned), F8),
            pltpu.VMEM((2 * halo, owned), BF16),
            pltpu.VMEM((2 * halo, owned), BF16),
            pltpu.VMEM((256, owned), BF16),
            pltpu.VMEM((owned, 2 * halo + 256), BF16),
            pltpu.VMEM((rows, owned), F32),
            pltpu.VMEM((rows, owned), F32),
            pltpu.VMEM((rows, owned), F32),
            pltpu.VMEM((2, 2 * rows, owned), BF16),
            pltpu.VMEM((2, 96, owned), F8),
            pltpu.VMEM((turns, n, count // 2, 128), F32),
            pltpu.VMEM((turns - 1, 2, rows, halo), F32),
            pltpu.VMEM((turns - 1, 2, rows, halo), F32),
            pltpu.SemaphoreType.DMA((3,)),
            pltpu.SemaphoreType.DMA((turns,)),
            pltpu.SemaphoreType.DMA((turns,)),
            pltpu.SemaphoreType.DMA((turns - 1, 2)),
            pltpu.SemaphoreType.DMA((turns - 1, 2)),
        ],
        compiler_params=pltpu.CompilerParams(
            collective_id=0, has_side_effects=True, vmem_limit_bytes=56 * 1024 * 1024
        ),
    )(
        jnp.transpose(adjoint_seed, (1, 0, 2)),
        inverse,
        jnp.transpose(flux_jacobians, (2, 3, 0, 1)),
        jnp.transpose(modal_shapes, (1, 0, 2)),
        modal_gain[None, :],
        face_cells,
        face_weights.reshape(nfaces // 128, 128),
        colours[None, :],
        send_cells,
    )
    out, part = pl.pallas_call(
        hand_over,
        out_shape=(
            jax.ShapeDtypeStruct((rows, owned), F32),
            jax.ShapeDtypeStruct((count, modes), F32),
        ),
        in_specs=[vmem, vmem],
        out_specs=(hbm, hbm),
        scratch_shapes=[
            pltpu.SemaphoreType.DMA((2,)),
        ],
    )(
        pltpu.with_memory_space_constraint(out, pltpu.VMEM),
        pltpu.with_memory_space_constraint(part, pltpu.VMEM),
    )
    return jnp.transpose(out.reshape(nvar, count, owned), (1, 0, 2)), part


def solution(mesh):
    return jax.shard_map(
        local,
        mesh=mesh,
        in_specs=(
            P("group", None, "cell"),
            P("group", None, None, "cell"),
            P(None, "group", None, None),
            P(None, None, "cell"),
            P("group"),
            P(None, "cell"),
            P("cell"),
            P("cell"),
            P(None, "cell"),
        ),
        out_specs=(P("group", None, "cell"), P("group", None)),
        check_vma=False,
    )
```

```python
import functools
import math

import jax
import jax.numpy as jnp
from jax import lax
from jax.experimental import pallas as pl
from jax.experimental.pallas import tpu as pltpu
from jax.sharding import PartitionSpec as P

ITERS = 4
FREQUENCY = 0.04
F32 = jnp.float32
BF16 = jnp.bfloat16
F8 = jnp.float8_e4m3fn
LIFT = 256.0
F8_MAX = 448.0
SPAN = 32.0
MODE_ROWS = 24
CANDIDATES = 40


def spectral_weights(count):
    return [FREQUENCY * 0.5 * (-1.0) ** d / math.tan(math.pi * d / count) for d in range(1, count)]


def bf16_factors(value):
    best_q = jnp.ones_like(value)
    best = jnp.abs(value - value.astype(BF16).astype(F32))
    for k in range(1, CANDIDATES):
        q = 1.0 + k / 128.0
        miss = jnp.abs(value - (value * (1.0 / q)).astype(BF16).astype(F32) * q)
        best_q = jnp.where(miss < best, q, best_q)
        best = jnp.minimum(miss, best)
    return (value / best_q).astype(BF16), best_q.astype(BF16)


def split(value):
    high = value.astype(BF16)
    return high, (value - high.astype(F32)).astype(BF16)


def split_f8(value):
    high = value.astype(BF16)
    low = (value - high.astype(F32)) * LIFT
    return high, jnp.clip(low, -F8_MAX, F8_MAX).astype(F8)


def mm(left, right):
    return jnp.dot(left, right, preferred_element_type=F32)


def mm_nt(left, right):
    return lax.dot_general(left, right, (((1,), (1,)), ((), ())), preferred_element_type=F32)


def kernel(
    n,
    seed_hbm,
    inv_hbm,
    flux_ref,
    shapes_hbm,
    gain_ref,
    faces_ref,
    g_ref,
    col_ref,
    send_ref,
    out_hbm,
    part_ref,
    seed_ref,
    inv_ref,
    shapes_ref,
    w_ref,
    gain_pad,
    left_hot,
    upper_hot,
    block_a,
    block_b,
    index_rows,
    value_rows,
    m_high,
    m_low,
    t_high,
    t_low,
    mg_high,
    mg_low,
    p_ref,
    sel_ref,
    x_ref,
    z_ref,
    base_ref,
    ab_ref,
    ab_low,
    q_all,
    ghost_out,
    ghost_in,
    in_sem,
    q_send,
    q_recv,
    g_send,
    g_recv,
):
    nvar, count, owned = seed_ref.shape
    modes = shapes_ref.shape[1]
    rows = count * nvar
    halo = send_ref.shape[1]
    nfaces = faces_ref.shape[1]
    me = lax.axis_index("cell")
    lower, upper = lax.rem(me + n - 1, n), lax.rem(me + 1, n)
    peers = partners(me, n)
    loads = [
        pltpu.make_async_copy(src, dst, in_sem.at[k])
        for k, (src, dst) in enumerate(
            [(seed_hbm, seed_ref), (shapes_hbm, shapes_ref), (inv_hbm, inv_ref)]
        )
    ]
    for load in loads:
        load.start()

    barrier = pltpu.get_barrier_semaphore()
    for d in range(1, n):
        pl.semaphore_signal(barrier, inc=1, device_id={"cell": peers[d]}, device_id_type=pl.DeviceIdType.MESH)

    left = faces_ref[0:1, :].astype(jnp.int16)
    right = faces_ref[1:2, :].astype(jnp.int16)
    p_tile, q_tile = bf16_factors(g_ref[...])
    p_tile, q_tile = p_tile.astype(F32), q_tile.astype(F32)
    p_row = jnp.concatenate([p_tile[k : k + 1, :] for k in range(nfaces // 128)], axis=1).astype(BF16)
    q_row = jnp.concatenate([q_tile[k : k + 1, :] for k in range(nfaces // 128)], axis=1).astype(BF16)
    step = 128
    wide = 256
    tall = owned + halo

    for k, row in enumerate((left, right)):
        index_rows[k] = jnp.broadcast_to(row, (16, nfaces))
    for k, row in enumerate((p_row, q_row)):
        value_rows[k] = jnp.broadcast_to(row, (16, nfaces))
    sixteen = lax.broadcasted_iota(jnp.int32, (16, 128), 0)

    def hot(side, start, size):
        near = index_rows[side]
        value = value_rows[side]
        zero = jnp.zeros((16, nfaces), BF16)
        strips = []
        for k in range(size // 16):
            line = (sixteen + (start + 16 * k)).astype(jnp.int16)
            strips.append(jnp.where(near == jnp.concatenate([line] * (nfaces // 128), axis=1), value, zero))
        return jnp.concatenate(strips, axis=0)

    cut = owned // 2

    def split_block(at, block_ref, r0, r1):
        here = pl.ds(at, wide)
        block = block_ref[0 : r1 - r0, :]
        high, low = split_f8(block)
        m_high[r0:r1, here] = high
        m_low[r0:r1, here] = low
        high, low = split_f8(block.T)
        t_high[here, r0:r1] = high
        t_low[here, r0:r1] = low

    @pl.loop(0, tall // step)
    def _(t):
        at = pl.multiple_of(t * step, step)
        left_hot[pl.ds(at, step), :] = hot(0, at, step)


    send_row = jnp.concatenate([send_ref[0:1, :], send_ref[1:2, :]], axis=1)
    loads[0].wait()
    loads[1].wait()

    @pl.loop(0, owned // wide)
    def _(t):
        at = pl.multiple_of(t * wide, wide)
        here = pl.ds(at, wide)
        sel_ref[here, 0 : 2 * halo] = jnp.where(
            send_row - at == lax.broadcasted_iota(jnp.int32, (wide, 2 * halo), 0), 1.0, 0.0
        ).astype(BF16)
        pad = jnp.zeros((MODE_ROWS - modes, wide), F32)
        lines = []
        for v in range(nvar):
            lines += [shapes_ref[v, :, here], pad]
            z_ref[v * count : (v + 1) * count, here] = seed_ref[v, :, here]
            base_ref[v * count : (v + 1) * count, here] = seed_ref[v, :, here]
        lines.append(jnp.zeros((128 - nvar * MODE_ROWS, wide), F32))
        high, low = split(jnp.concatenate(lines, axis=0))
        p_ref[0:128, here] = high
        p_ref[128:256, here] = low
        sel_ref[here, 2 * halo : 2 * halo + 128] = high.astype(F32).T.astype(BF16)
        sel_ref[here, 2 * halo + 128 :] = low.astype(F32).T.astype(BF16)
        eye_line = lax.broadcasted_iota(jnp.int32, (count, rows), 0)
        eye_lane = lax.broadcasted_iota(jnp.int32, (count, rows), 1)
        eye = lax.rem(eye_lane, count) == eye_line
        blocks = []
        for side in range(2):
            for w in range(nvar):
                row = jnp.concatenate([flux_ref[v, w][side : side + 1, :] for v in range(nvar)], axis=1)
                blocks.append(jnp.where(eye, jnp.broadcast_to(row, (count, rows)), 0.0))
        line = lax.broadcasted_iota(jnp.int32, (rows, rows), 0)
        lane = lax.broadcasted_iota(jnp.int32, (rows, rows), 1)
        apart = lax.rem(lane, count) - lax.rem(line, count)
        spectral = jnp.zeros((rows, rows), F32)
        for d, weight in enumerate(spectral_weights(count), 1):
            spectral = jnp.where(apart == d, weight, jnp.where(apart == -d, -weight, spectral))
        spectral = jnp.where(lax.div(lane, count) == lax.div(line, count), spectral, 0.0)
        w_high, w_low = split(jnp.concatenate(blocks + [spectral], axis=0))
        lane = lax.broadcasted_iota(jnp.int32, (rows, 3 * rows), 1)
        line = lax.broadcasted_iota(jnp.int32, (rows, 3 * rows), 0)
        first = jnp.where((lane == line) | (lane == line + rows), 1.0, 0.0).astype(BF16)
        last = jnp.where(lane == line + 2 * rows, 1.0, 0.0).astype(BF16)
        w_ref[...] = (mm(w_high, first) + mm(w_low, last)).astype(BF16)
        right_now = hot(1, at, wide)
        earlier = lax.rem(t + owned // wide - 1, owned // wide)
        split_block(pl.multiple_of(earlier * wide, wide), block_b, 0, cut)
        block_a[...] = mm_nt(left_hot[cut:tall, :], right_now)
        split_block(at, block_a, cut, owned)
        high, low = split(block_a[owned - cut : tall - cut, :])
        mg_high[0:halo, here] = high
        mg_low[0:halo, here] = low
        block_b[...] = mm_nt(left_hot[0:cut, :], right_now)

    split_block(owned - wide, block_b, 0, cut)

    def build_ghost_matrix():
        upper_hot[...] = hot(1, owned + halo, halo)

        @pl.loop(0, owned // wide)
        def _(t):
            at = pl.multiple_of(t * wide, wide)
            high, low = split(mm_nt(upper_hot[...], left_hot[pl.ds(at, wide), :]))
            mg_high[halo:, pl.ds(at, wide)] = high
            mg_low[halo:, pl.ds(at, wide)] = low

    loads[2].wait()
    gain_pad[...] = jnp.zeros((1, 128), F32)
    gain_pad[:, 0:modes] = gain_ref[...]
    colours = col_ref[...]

    def update(colour):
        mask = colours == colour
        for w in range(nvar):
            spot = slice(w * count, (w + 1) * count)
            total = inv_ref[0, w].astype(F32) * z_ref[0:count, :]
            for v in range(1, nvar):
                total = total + inv_ref[v, w].astype(F32) * z_ref[v * count : (v + 1) * count, :]
            x_ref[spot, :] = jnp.where(mask, total, x_ref[spot, :])

    def coupling():
        value = x_ref[...]
        top = jnp.max(jnp.abs(value), axis=0, keepdims=True)
        top = jnp.maximum(jnp.max(top, axis=1, keepdims=True), 1e-30)
        scale = SPAN / top
        high, low = split(value)
        both = mm(w_ref[...], jnp.concatenate([high, low, high], axis=0))
        for side in range(2):
            part = both[side * rows : (side + 1) * rows]
            high, low = split(part)
            ab_ref[side, 0:rows, :] = high
            ab_ref[side, rows:, :] = low
            rough = jnp.concatenate([part * scale, jnp.zeros((96 - rows, owned), F32)], axis=0)
            ab_low[side] = rough.astype(F8)
        one = mm(ab_ref[0], m_high[...]) + mm(ab_ref[1], t_high[...])
        two = mm(ab_low[0], m_low[...]) + mm(ab_low[1], t_low[...])
        z_ref[...] = both[2 * rows :] + (one[:rows] + one[rows:] + two[:rows] * (top * (1.0 / (SPAN * LIFT))))

    def modal_copies(turn):
        return [
            pltpu.make_async_remote_copy(
                src_ref=q_all.at[turn, me],
                dst_ref=q_all.at[turn, me],
                send_sem=q_send.at[turn],
                recv_sem=q_recv.at[turn],
                device_id={"cell": peers[d]},
                device_id_type=pl.DeviceIdType.MESH,
            )
            for d in range(n - 1, 0, -1)
        ]

    def wait_modal(turn):
        every = q_all.at[turn, pl.ds(0, n - 1)]
        pltpu.make_async_copy(every, every, q_send.at[turn]).wait()
        pltpu.make_async_copy(every, every, q_recv.at[turn]).wait()

    def ghost_copies(turn):
        return [
            pltpu.make_async_remote_copy(
                src_ref=ghost_out.at[turn, way],
                dst_ref=ghost_in.at[turn, 1 - way],
                send_sem=g_send.at[turn, way],
                recv_sem=g_recv.at[turn, way],
                device_id={"cell": lower if way == 0 else upper},
                device_id_type=pl.DeviceIdType.MESH,
            )
            for way in range(2)
        ]

    def start_exchange(turn):
        high, low = split(x_ref[...])
        every = mm(jnp.concatenate([high, low], axis=0), sel_ref[...])
        every = every[:rows] + every[rows:]
        @pl.when(turn == 0)
        def _():
            pl.semaphore_wait(barrier, n - 1)

        @pl.when(turn < ITERS - 1)
        def _():
            ghost_out[turn, 0] = every[:, :halo]
            ghost_out[turn, 1] = every[:, halo : 2 * halo]
            for copy in ghost_copies(turn):
                copy.start()

        gram = every[:, 2 * halo : 2 * halo + 128] + every[:, 2 * halo + 128 :]
        part = gram[0:count, 0:MODE_ROWS]
        for v in range(1, nvar):
            part = part + gram[v * count : (v + 1) * count, v * MODE_ROWS : (v + 1) * MODE_ROWS]
        size = count // 4
        pieces = [part[k * size : (k + 1) * size] for k in range(4)]
        q_all[turn, me] = jnp.concatenate(pieces + [jnp.zeros((size, 128 - 4 * MODE_ROWS), F32)], axis=1)
        for copy in modal_copies(turn):
            copy.start()

    def modal_sum(turn):
        total = q_all[turn, 0]
        for d in range(1, n):
            total = total + q_all[turn, d]
        return jnp.concatenate([total[:, k * MODE_ROWS : (k + 1) * MODE_ROWS] for k in range(4)], axis=0)

    x_ref[...] = jnp.zeros((rows, owned), F32)
    @pl.loop(0, ITERS)
    def _(sweep):
        @pl.when(sweep > 0)
        def _():
            coupling()

            @pl.when(sweep == 1)
            def _():
                build_ghost_matrix()

            for copy in ghost_copies(sweep - 1):
                copy.wait()
            wait_modal(sweep - 1)
            low_part = ghost_in[sweep - 1, 0]
            up_part = ghost_in[sweep - 1, 1]
            high, low = split(jnp.concatenate([low_part, up_part], axis=1))
            both = mm(w_ref[0 : 2 * rows, :], jnp.concatenate([high, low, high], axis=0))
            ghost_ab = jnp.concatenate([both[:rows, :halo], both[rows:, halo:]], axis=1)
            ghost_high, ghost_low = split(ghost_ab)
            lam = modal_sum(sweep - 1) * gain_pad[:, :MODE_ROWS]
            lam = jnp.concatenate([lam] * nvar + [jnp.zeros((count, 128 - nvar * MODE_ROWS), F32)], axis=1)
            lam = jnp.concatenate([lam] * nvar, axis=0)
            lane = lax.broadcasted_iota(jnp.int32, (rows, 128), 1)
            line = lax.broadcasted_iota(jnp.int32, (rows, 128), 0)
            lam = jnp.where(lax.div(lane, MODE_ROWS) == lax.div(line, count), -lam, 0.0)
            lam_high, lam_low = split(lam)
            term = mm(jnp.concatenate([ghost_high, ghost_low], axis=0), mg_high[...]) + mm(
                jnp.concatenate([lam_high, lam_low], axis=0), p_ref[0:128, :]
            )
            rest = mm(ghost_high, mg_low[...]) + mm(lam_high, p_ref[128:256, :])
            term = term[:rows] + term[rows:] + rest
            for v in range(nvar):
                spot = slice(v * count, (v + 1) * count)
                base = seed_ref[v] - term[spot]
                base_ref[spot, :] = base
                z_ref[spot, :] = base - z_ref[spot, :]

        update(0)
        coupling()
        z_ref[...] = base_ref[...] - z_ref[...]
        update(1)
        start_exchange(sweep)

    out_hbm[...] = x_ref[...]
    wait_modal(ITERS - 1)
    part_ref[...] = modal_sum(ITERS - 1)[:, :modes]


def partners(me, n):
    if n & (n - 1):
        return [lax.rem(me + d, n) for d in range(n)]
    places = []
    for d in range(n):
        place = me
        bit = 1
        while bit < n:
            if d & bit:
                place = place + bit - 2 * bit * lax.rem(lax.div(me, bit), 2)
            bit *= 2
        places.append(place)
    return places


def hand_over(out_ref, part_ref, out_final, part_final, sem):
    first = pltpu.make_async_copy(out_ref, out_final, sem.at[0])
    second = pltpu.make_async_copy(part_ref, part_final, sem.at[1])
    first.start()
    second.start()
    first.wait()
    second.wait()


def local(
    adjoint_seed,
    inv_blocks,
    flux_jacobians,
    modal_shapes,
    modal_gain,
    face_cells,
    face_weights,
    colours,
    send_cells,
):
    n = lax.axis_size("cell")
    count, nvar, owned = adjoint_seed.shape
    modes = modal_shapes.shape[0]
    rows = count * nvar
    halo = send_cells.shape[1]
    nfaces = face_weights.shape[0]
    inverse = jnp.transpose(inv_blocks, (1, 2, 0, 3))
    vmem = pl.BlockSpec(memory_space=pltpu.VMEM)
    hbm = pl.BlockSpec(memory_space=pl.ANY)
    tall = owned + halo
    turns = ITERS
    out, part = pl.pallas_call(
        functools.partial(kernel, n),
        out_shape=(
            pltpu.VMEM((rows, owned), F32),
            pltpu.VMEM((count, modes), F32),
        ),
        in_specs=[hbm, hbm, vmem, hbm] + [vmem] * 5,
        out_specs=(vmem, vmem),
        scratch_shapes=[
            pltpu.VMEM((nvar, count, owned), F32),
            pltpu.VMEM((nvar, nvar, count, owned), BF16),
            pltpu.VMEM((nvar, modes, owned), F32),
            pltpu.VMEM((3 * rows, 3 * rows), BF16),
            pltpu.VMEM((1, 128), F32),
            pltpu.VMEM((tall, nfaces), BF16),
            pltpu.VMEM((halo, nfaces), BF16),
            pltpu.VMEM((owned // 2 + halo, 256), F32),
            pltpu.VMEM((owned // 2, 256), F32),
            pltpu.VMEM((2, 16, nfaces), jnp.int16),
            pltpu.VMEM((2, 16, nfaces), BF16),
            pltpu.VMEM((owned, owned), BF16),
            pltpu.VMEM((owned, owned), F8),
            pltpu.VMEM((owned, owned), BF16),
            pltpu.VMEM((owned, owned), F8),
            pltpu.VMEM((2 * halo, owned), BF16),
            pltpu.VMEM((2 * halo, owned), BF16),
            pltpu.VMEM((256, owned), BF16),
            pltpu.VMEM((owned, 2 * halo + 256), BF16),
            pltpu.VMEM((rows, owned), F32),
            pltpu.VMEM((rows, owned), F32),
            pltpu.VMEM((rows, owned), F32),
            pltpu.VMEM((2, 2 * rows, owned), BF16),
            pltpu.VMEM((2, 96, owned), F8),
            pltpu.VMEM((turns, n, count // 4, 128), F32),
            pltpu.VMEM((turns - 1, 2, rows, halo), F32),
            pltpu.VMEM((turns - 1, 2, rows, halo), F32),
            pltpu.SemaphoreType.DMA((3,)),
            pltpu.SemaphoreType.DMA((turns,)),
            pltpu.SemaphoreType.DMA((turns,)),
            pltpu.SemaphoreType.DMA((turns - 1, 2)),
            pltpu.SemaphoreType.DMA((turns - 1, 2)),
        ],
        compiler_params=pltpu.CompilerParams(
            collective_id=0, has_side_effects=True, vmem_limit_bytes=56 * 1024 * 1024
        ),
    )(
        jnp.transpose(adjoint_seed, (1, 0, 2)),
        inverse,
        jnp.transpose(flux_jacobians, (2, 3, 0, 1)),
        jnp.transpose(modal_shapes, (1, 0, 2)),
        modal_gain[None, :],
        face_cells,
        face_weights.reshape(nfaces // 128, 128),
        colours[None, :],
        send_cells,
    )
    out, part = pl.pallas_call(
        hand_over,
        out_shape=(
            jax.ShapeDtypeStruct((rows, owned), F32),
            jax.ShapeDtypeStruct((count, modes), F32),
        ),
        in_specs=[vmem, vmem],
        out_specs=(hbm, hbm),
        scratch_shapes=[
            pltpu.SemaphoreType.DMA((2,)),
        ],
    )(
        pltpu.with_memory_space_constraint(out, pltpu.VMEM),
        pltpu.with_memory_space_constraint(part, pltpu.VMEM),
    )
    return jnp.transpose(out.reshape(nvar, count, owned), (1, 0, 2)), part


def solution(mesh):
    return jax.shard_map(
        local,
        mesh=mesh,
        in_specs=(
            P("group", None, "cell"),
            P("group", None, None, "cell"),
            P(None, "group", None, None),
            P(None, None, "cell"),
            P("group"),
            P(None, "cell"),
            P("cell"),
            P("cell"),
            P(None, "cell"),
        ),
        out_specs=(P("group", None, "cell"), P("group", None)),
        check_vma=False,
    )
```

```python
import functools
import math

import jax
import jax.numpy as jnp
from jax import lax
from jax.experimental import pallas as pl
from jax.experimental.pallas import tpu as pltpu
from jax.sharding import PartitionSpec as P

ITERS = 4
FREQUENCY = 0.04
F32 = jnp.float32
BF16 = jnp.bfloat16
F8 = jnp.float8_e4m3fn
LIFT = 256.0
F8_MAX = 448.0
SPAN = 32.0
MODE_ROWS = 24
CANDIDATES = 40


def spectral_weights(count):
    return [FREQUENCY * 0.5 * (-1.0) ** d / math.tan(math.pi * d / count) for d in range(1, count)]


def bf16_factors(value):
    best_q = jnp.ones_like(value)
    best = jnp.abs(value - value.astype(BF16).astype(F32))
    for k in range(1, CANDIDATES):
        q = 1.0 + k / 128.0
        miss = jnp.abs(value - (value * (1.0 / q)).astype(BF16).astype(F32) * q)
        best_q = jnp.where(miss < best, q, best_q)
        best = jnp.minimum(miss, best)
    return (value / best_q).astype(BF16), best_q.astype(BF16)


def split(value):
    high = value.astype(BF16)
    return high, (value - high.astype(F32)).astype(BF16)


def split_f8(value):
    high = value.astype(BF16)
    low = (value - high.astype(F32)) * LIFT
    return high, jnp.clip(low, -F8_MAX, F8_MAX).astype(F8)


def mm(left, right):
    return jnp.dot(left, right, preferred_element_type=F32)


def mm_nt(left, right):
    return lax.dot_general(left, right, (((1,), (1,)), ((), ())), preferred_element_type=F32)


def kernel(
    n,
    seed_hbm,
    inv_hbm,
    flux_ref,
    shapes_hbm,
    gain_ref,
    faces_ref,
    g_ref,
    col_ref,
    send_ref,
    out_hbm,
    part_ref,
    seed_ref,
    inv_ref,
    shapes_ref,
    w_ref,
    gain_pad,
    left_hot,
    upper_hot,
    block_a,
    block_b,
    index_rows,
    value_rows,
    m_high,
    m_low,
    t_high,
    t_low,
    mg_high,
    mg_low,
    p_ref,
    sel_ref,
    x_ref,
    z_ref,
    base_ref,
    ab_ref,
    ab_low,
    q_all,
    ghost_out,
    ghost_in,
    in_sem,
    q_send,
    q_recv,
    g_send,
    g_recv,
):
    nvar, count, owned = seed_ref.shape
    modes = shapes_ref.shape[1]
    rows = count * nvar
    halo = send_ref.shape[1]
    nfaces = faces_ref.shape[1]
    me = lax.axis_index("cell")
    lower, upper = lax.rem(me + n - 1, n), lax.rem(me + 1, n)
    peers = partners(me, n)
    loads = [
        pltpu.make_async_copy(src, dst, in_sem.at[k])
        for k, (src, dst) in enumerate(
            [(seed_hbm, seed_ref), (shapes_hbm, shapes_ref), (inv_hbm, inv_ref)]
        )
    ]
    for load in loads:
        load.start()

    barrier = pltpu.get_barrier_semaphore()
    for d in range(1, n):
        pl.semaphore_signal(barrier, inc=1, device_id={"cell": peers[d]}, device_id_type=pl.DeviceIdType.MESH)

    left = faces_ref[0:1, :].astype(jnp.int16)
    right = faces_ref[1:2, :].astype(jnp.int16)
    p_tile, q_tile = bf16_factors(g_ref[...])
    p_tile, q_tile = p_tile.astype(F32), q_tile.astype(F32)
    p_row = jnp.concatenate([p_tile[k : k + 1, :] for k in range(nfaces // 128)], axis=1).astype(BF16)
    q_row = jnp.concatenate([q_tile[k : k + 1, :] for k in range(nfaces // 128)], axis=1).astype(BF16)
    step = 128
    wide = 256
    tall = owned + halo

    for k, row in enumerate((left, right)):
        index_rows[k] = jnp.broadcast_to(row, (16, nfaces))
    for k, row in enumerate((p_row, q_row)):
        value_rows[k] = jnp.broadcast_to(row, (16, nfaces))
    sixteen = lax.broadcasted_iota(jnp.int32, (16, 128), 0)

    def hot(side, start, size):
        near = index_rows[side]
        value = value_rows[side]
        zero = jnp.zeros((16, nfaces), BF16)
        strips = []
        for k in range(size // 16):
            line = (sixteen + (start + 16 * k)).astype(jnp.int16)
            strips.append(jnp.where(near == jnp.concatenate([line] * (nfaces // 128), axis=1), value, zero))
        return jnp.concatenate(strips, axis=0)

    cut = owned // 2

    def split_block(at, block_ref, r0, r1):
        here = pl.ds(at, wide)
        block = block_ref[0 : r1 - r0, :]
        high, low = split_f8(block)
        m_high[r0:r1, here] = high
        m_low[r0:r1, here] = low
        high, low = split_f8(block.T)
        t_high[here, r0:r1] = high
        t_low[here, r0:r1] = low

    @pl.loop(0, tall // step)
    def _(t):
        at = pl.multiple_of(t * step, step)
        left_hot[pl.ds(at, step), :] = hot(0, at, step)


    send_row = jnp.concatenate([send_ref[0:1, :], send_ref[1:2, :]], axis=1)
    loads[0].wait()
    loads[1].wait()

    @pl.loop(0, owned // wide)
    def _(t):
        at = pl.multiple_of(t * wide, wide)
        here = pl.ds(at, wide)
        sel_ref[here, 0 : 2 * halo] = jnp.where(
            send_row - at == lax.broadcasted_iota(jnp.int32, (wide, 2 * halo), 0), 1.0, 0.0
        ).astype(BF16)
        pad = jnp.zeros((MODE_ROWS - modes, wide), F32)
        lines = []
        for v in range(nvar):
            lines += [shapes_ref[v, :, here], pad]
            z_ref[v * count : (v + 1) * count, here] = seed_ref[v, :, here]
            base_ref[v * count : (v + 1) * count, here] = seed_ref[v, :, here]
        lines.append(jnp.zeros((128 - nvar * MODE_ROWS, wide), F32))
        high, low = split(jnp.concatenate(lines, axis=0))
        p_ref[0:128, here] = high
        p_ref[128:256, here] = low
        sel_ref[here, 2 * halo : 2 * halo + 128] = high.astype(F32).T.astype(BF16)
        sel_ref[here, 2 * halo + 128 :] = low.astype(F32).T.astype(BF16)
        eye_line = lax.broadcasted_iota(jnp.int32, (count, rows), 0)
        eye_lane = lax.broadcasted_iota(jnp.int32, (count, rows), 1)
        eye = lax.rem(eye_lane, count) == eye_line
        blocks = []
        for side in range(2):
            for w in range(nvar):
                row = jnp.concatenate([flux_ref[v, w][side : side + 1, :] for v in range(nvar)], axis=1)
                blocks.append(jnp.where(eye, jnp.broadcast_to(row, (count, rows)), 0.0))
        line = lax.broadcasted_iota(jnp.int32, (rows, rows), 0)
        lane = lax.broadcasted_iota(jnp.int32, (rows, rows), 1)
        apart = lax.rem(lane, count) - lax.rem(line, count)
        spectral = jnp.zeros((rows, rows), F32)
        for d, weight in enumerate(spectral_weights(count), 1):
            spectral = jnp.where(apart == d, weight, jnp.where(apart == -d, -weight, spectral))
        spectral = jnp.where(lax.div(lane, count) == lax.div(line, count), spectral, 0.0)
        w_high, w_low = split(jnp.concatenate(blocks + [spectral], axis=0))
        lane = lax.broadcasted_iota(jnp.int32, (rows, 3 * rows), 1)
        line = lax.broadcasted_iota(jnp.int32, (rows, 3 * rows), 0)
        first = jnp.where((lane == line) | (lane == line + rows), 1.0, 0.0).astype(BF16)
        last = jnp.where(lane == line + 2 * rows, 1.0, 0.0).astype(BF16)
        w_ref[...] = (mm(w_high, first) + mm(w_low, last)).astype(BF16)
        right_now = hot(1, at, wide)
        earlier = lax.rem(t + owned // wide - 1, owned // wide)
        split_block(pl.multiple_of(earlier * wide, wide), block_b, 0, cut)
        block_a[...] = mm_nt(left_hot[cut:tall, :], right_now)
        split_block(at, block_a, cut, owned)
        high, low = split(block_a[owned - cut : tall - cut, :])
        mg_high[0:halo, here] = high
        mg_low[0:halo, here] = low
        block_b[...] = mm_nt(left_hot[0:cut, :], right_now)

    split_block(owned - wide, block_b, 0, cut)

    def build_ghost_matrix():
        upper_hot[...] = hot(1, owned + halo, halo)

        @pl.loop(0, owned // wide)
        def _(t):
            at = pl.multiple_of(t * wide, wide)
            high, low = split(mm_nt(upper_hot[...], left_hot[pl.ds(at, wide), :]))
            mg_high[halo:, pl.ds(at, wide)] = high
            mg_low[halo:, pl.ds(at, wide)] = low

    loads[2].wait()
    gain_pad[...] = jnp.zeros((1, 128), F32)
    gain_pad[:, 0:modes] = gain_ref[...]
    colours = col_ref[...]

    def update(colour):
        mask = colours == colour
        for w in range(nvar):
            spot = slice(w * count, (w + 1) * count)
            total = inv_ref[0, w].astype(F32) * z_ref[0:count, :]
            for v in range(1, nvar):
                total = total + inv_ref[v, w].astype(F32) * z_ref[v * count : (v + 1) * count, :]
            x_ref[spot, :] = jnp.where(mask, total, x_ref[spot, :])

    def coupling():
        value = x_ref[...]
        top = jnp.max(jnp.abs(value), axis=0, keepdims=True)
        top = jnp.maximum(jnp.max(top, axis=1, keepdims=True), 1e-30)
        scale = SPAN / top
        high, low = split(value)
        both = mm(w_ref[...], jnp.concatenate([high, low, high], axis=0))
        for side in range(2):
            part = both[side * rows : (side + 1) * rows]
            high, low = split(part)
            ab_ref[side, 0:rows, :] = high
            ab_ref[side, rows:, :] = low
            rough = jnp.concatenate([part * scale, jnp.zeros((96 - rows, owned), F32)], axis=0)
            ab_low[side] = rough.astype(F8)
        one = mm(ab_ref[0], m_high[...]) + mm(ab_ref[1], t_high[...])
        two = mm(ab_low[0], m_low[...]) + mm(ab_low[1], t_low[...])
        z_ref[...] = both[2 * rows :] + (one[:rows] + one[rows:] + two[:rows] * (top * (1.0 / (SPAN * LIFT))))

    def modal_copies(turn):
        return [
            pltpu.make_async_remote_copy(
                src_ref=q_all.at[turn, me],
                dst_ref=q_all.at[turn, me],
                send_sem=q_send.at[turn],
                recv_sem=q_recv.at[turn],
                device_id={"cell": peers[d]},
                device_id_type=pl.DeviceIdType.MESH,
            )
            for d in range(n - 1, 0, -1)
        ]

    def wait_modal(turn):
        every = q_all.at[turn, pl.ds(0, n - 1)]
        pltpu.make_async_copy(every, every, q_recv.at[turn]).wait()

    def ghost_copies(turn):
        return [
            pltpu.make_async_remote_copy(
                src_ref=ghost_out.at[turn, way],
                dst_ref=ghost_in.at[turn, 1 - way],
                send_sem=g_send.at[turn, way],
                recv_sem=g_recv.at[turn, way],
                device_id={"cell": lower if way == 0 else upper},
                device_id_type=pl.DeviceIdType.MESH,
            )
            for way in range(2)
        ]

    def start_exchange(turn):
        high, low = split(x_ref[...])
        every = mm(jnp.concatenate([high, low], axis=0), sel_ref[...])
        every = every[:rows] + every[rows:]
        @pl.when(turn == 0)
        def _():
            pl.semaphore_wait(barrier, n - 1)

        @pl.when(turn < ITERS - 1)
        def _():
            ghost_out[turn, 0] = every[:, :halo]
            ghost_out[turn, 1] = every[:, halo : 2 * halo]
            for copy in ghost_copies(turn):
                copy.start()

        gram = every[:, 2 * halo : 2 * halo + 128] + every[:, 2 * halo + 128 :]
        part = gram[0:count, 0:MODE_ROWS]
        for v in range(1, nvar):
            part = part + gram[v * count : (v + 1) * count, v * MODE_ROWS : (v + 1) * MODE_ROWS]
        size = count // 4
        pieces = [part[k * size : (k + 1) * size] for k in range(4)]
        q_all[turn, me] = jnp.concatenate(pieces + [jnp.zeros((size, 128 - 4 * MODE_ROWS), F32)], axis=1)
        for copy in modal_copies(turn):
            copy.start()

    def modal_sum(turn):
        total = q_all[turn, 0]
        for d in range(1, n):
            total = total + q_all[turn, d]
        return jnp.concatenate([total[:, k * MODE_ROWS : (k + 1) * MODE_ROWS] for k in range(4)], axis=0)

    x_ref[...] = jnp.zeros((rows, owned), F32)
    @pl.loop(0, ITERS)
    def _(sweep):
        @pl.when(sweep > 0)
        def _():
            coupling()

            @pl.when(sweep == 1)
            def _():
                build_ghost_matrix()

            for copy in ghost_copies(sweep - 1):
                copy.wait_recv()
            wait_modal(sweep - 1)
            low_part = ghost_in[sweep - 1, 0]
            up_part = ghost_in[sweep - 1, 1]
            high, low = split(jnp.concatenate([low_part, up_part], axis=1))
            both = mm(w_ref[0 : 2 * rows, :], jnp.concatenate([high, low, high], axis=0))
            ghost_ab = jnp.concatenate([both[:rows, :halo], both[rows:, halo:]], axis=1)
            ghost_high, ghost_low = split(ghost_ab)
            lam = modal_sum(sweep - 1) * gain_pad[:, :MODE_ROWS]
            lam = jnp.concatenate([lam] * nvar + [jnp.zeros((count, 128 - nvar * MODE_ROWS), F32)], axis=1)
            lam = jnp.concatenate([lam] * nvar, axis=0)
            lane = lax.broadcasted_iota(jnp.int32, (rows, 128), 1)
            line = lax.broadcasted_iota(jnp.int32, (rows, 128), 0)
            lam = jnp.where(lax.div(lane, MODE_ROWS) == lax.div(line, count), -lam, 0.0)
            lam_high, lam_low = split(lam)
            term = mm(jnp.concatenate([ghost_high, ghost_low], axis=0), mg_high[...]) + mm(
                jnp.concatenate([lam_high, lam_low], axis=0), p_ref[0:128, :]
            )
            rest = mm(ghost_high, mg_low[...]) + mm(lam_high, p_ref[128:256, :])
            term = term[:rows] + term[rows:] + rest
            for v in range(nvar):
                spot = slice(v * count, (v + 1) * count)
                base = seed_ref[v] - term[spot]
                base_ref[spot, :] = base
                z_ref[spot, :] = base - z_ref[spot, :]
            update(0)

        @pl.when(sweep == 0)
        def _():
            update(0)

        coupling()
        z_ref[...] = base_ref[...] - z_ref[...]
        update(1)
        start_exchange(sweep)

    out_hbm[...] = x_ref[...]
    for turn in range(ITERS):
        every = q_all.at[turn, pl.ds(0, n - 1)]
        pltpu.make_async_copy(every, every, q_send.at[turn]).wait()
        if turn < ITERS - 1:
            for copy in ghost_copies(turn):
                copy.wait_send()
    wait_modal(ITERS - 1)
    part_ref[...] = modal_sum(ITERS - 1)[:, :modes]


def partners(me, n):
    if n & (n - 1):
        return [lax.rem(me + d, n) for d in range(n)]
    places = []
    for d in range(n):
        place = me
        bit = 1
        while bit < n:
            if d & bit:
                place = place + bit - 2 * bit * lax.rem(lax.div(me, bit), 2)
            bit *= 2
        places.append(place)
    return places


def hand_over(out_ref, part_ref, out_final, part_final, sem):
    first = pltpu.make_async_copy(out_ref, out_final, sem.at[0])
    second = pltpu.make_async_copy(part_ref, part_final, sem.at[1])
    first.start()
    second.start()
    first.wait()
    second.wait()


def local(
    adjoint_seed,
    inv_blocks,
    flux_jacobians,
    modal_shapes,
    modal_gain,
    face_cells,
    face_weights,
    colours,
    send_cells,
):
    n = lax.axis_size("cell")
    count, nvar, owned = adjoint_seed.shape
    modes = modal_shapes.shape[0]
    rows = count * nvar
    halo = send_cells.shape[1]
    nfaces = face_weights.shape[0]
    inverse = jnp.transpose(inv_blocks, (1, 2, 0, 3))
    vmem = pl.BlockSpec(memory_space=pltpu.VMEM)
    hbm = pl.BlockSpec(memory_space=pl.ANY)
    tall = owned + halo
    turns = ITERS
    out, part = pl.pallas_call(
        functools.partial(kernel, n),
        out_shape=(
            pltpu.VMEM((rows, owned), F32),
            pltpu.VMEM((count, modes), F32),
        ),
        in_specs=[hbm, hbm, vmem, hbm] + [vmem] * 5,
        out_specs=(vmem, vmem),
        scratch_shapes=[
            pltpu.VMEM((nvar, count, owned), F32),
            pltpu.VMEM((nvar, nvar, count, owned), BF16),
            pltpu.VMEM((nvar, modes, owned), F32),
            pltpu.VMEM((3 * rows, 3 * rows), BF16),
            pltpu.VMEM((1, 128), F32),
            pltpu.VMEM((tall, nfaces), BF16),
            pltpu.VMEM((halo, nfaces), BF16),
            pltpu.VMEM((owned // 2 + halo, 256), F32),
            pltpu.VMEM((owned // 2, 256), F32),
            pltpu.VMEM((2, 16, nfaces), jnp.int16),
            pltpu.VMEM((2, 16, nfaces), BF16),
            pltpu.VMEM((owned, owned), BF16),
            pltpu.VMEM((owned, owned), F8),
            pltpu.VMEM((owned, owned), BF16),
            pltpu.VMEM((owned, owned), F8),
            pltpu.VMEM((2 * halo, owned), BF16),
            pltpu.VMEM((2 * halo, owned), BF16),
            pltpu.VMEM((256, owned), BF16),
            pltpu.VMEM((owned, 2 * halo + 256), BF16),
            pltpu.VMEM((rows, owned), F32),
            pltpu.VMEM((rows, owned), F32),
            pltpu.VMEM((rows, owned), F32),
            pltpu.VMEM((2, 2 * rows, owned), BF16),
            pltpu.VMEM((2, 96, owned), F8),
            pltpu.VMEM((turns, n, count // 4, 128), F32),
            pltpu.VMEM((turns - 1, 2, rows, halo), F32),
            pltpu.VMEM((turns - 1, 2, rows, halo), F32),
            pltpu.SemaphoreType.DMA((3,)),
            pltpu.SemaphoreType.DMA((turns,)),
            pltpu.SemaphoreType.DMA((turns,)),
            pltpu.SemaphoreType.DMA((turns - 1, 2)),
            pltpu.SemaphoreType.DMA((turns - 1, 2)),
        ],
        compiler_params=pltpu.CompilerParams(
            collective_id=0, has_side_effects=True, vmem_limit_bytes=56 * 1024 * 1024
        ),
    )(
        jnp.transpose(adjoint_seed, (1, 0, 2)),
        inverse,
        jnp.transpose(flux_jacobians, (2, 3, 0, 1)),
        jnp.transpose(modal_shapes, (1, 0, 2)),
        modal_gain[None, :],
        face_cells,
        face_weights.reshape(nfaces // 128, 128),
        colours[None, :],
        send_cells,
    )
    out, part = pl.pallas_call(
        hand_over,
        out_shape=(
            jax.ShapeDtypeStruct((rows, owned), F32),
            jax.ShapeDtypeStruct((count, modes), F32),
        ),
        in_specs=[vmem, vmem],
        out_specs=(hbm, hbm),
        scratch_shapes=[
            pltpu.SemaphoreType.DMA((2,)),
        ],
    )(
        pltpu.with_memory_space_constraint(out, pltpu.VMEM),
        pltpu.with_memory_space_constraint(part, pltpu.VMEM),
    )
    return jnp.transpose(out.reshape(nvar, count, owned), (1, 0, 2)), part


def solution(mesh):
    return jax.shard_map(
        local,
        mesh=mesh,
        in_specs=(
            P("group", None, "cell"),
            P("group", None, None, "cell"),
            P(None, "group", None, None),
            P(None, None, "cell"),
            P("group"),
            P(None, "cell"),
            P("cell"),
            P("cell"),
            P(None, "cell"),
        ),
        out_specs=(P("group", None, "cell"), P("group", None)),
        check_vma=False,
    )
```

```python
import functools
import math

import jax
import jax.numpy as jnp
from jax import lax
from jax.experimental import pallas as pl
from jax.experimental.pallas import tpu as pltpu
from jax.sharding import PartitionSpec as P

ITERS = 4
FREQUENCY = 0.04
F32 = jnp.float32
BF16 = jnp.bfloat16
F8 = jnp.float8_e4m3fn
LIFT = 256.0
F8_MAX = 448.0
SPAN = 32.0
MODE_ROWS = 24
CANDIDATES = 40


def spectral_weights(count):
    return [FREQUENCY * 0.5 * (-1.0) ** d / math.tan(math.pi * d / count) for d in range(1, count)]


def bf16_factors(value):
    best_q = jnp.ones_like(value)
    best = jnp.abs(value - value.astype(BF16).astype(F32))

    def group(turn, state):
        best, best_q = state
        first = turn.astype(F32) * (8.0 / 128.0) + 1.0
        for k in range(8):
            q = first + k / 128.0
            miss = jnp.abs(value - (value / q).astype(BF16).astype(F32) * q)
            best_q = jnp.where(miss < best, q, best_q)
            best = jnp.minimum(miss, best)
        return best, best_q

    best, best_q = lax.fori_loop(0, CANDIDATES // 8, group, (best, best_q))
    return (value / best_q).astype(BF16), best_q.astype(BF16)


def split(value):
    high = value.astype(BF16)
    return high, (value - high.astype(F32)).astype(BF16)


def split_f8(value):
    high = value.astype(BF16)
    low = (value - high.astype(F32)) * LIFT
    return high, jnp.clip(low, -F8_MAX, F8_MAX).astype(F8)


def mm(left, right):
    return jnp.dot(left, right, preferred_element_type=F32)


def mm_nt(left, right):
    return lax.dot_general(left, right, (((1,), (1,)), ((), ())), preferred_element_type=F32)


def kernel(
    n,
    seed_hbm,
    inv_hbm,
    flux_ref,
    shapes_hbm,
    gain_ref,
    faces_ref,
    g_ref,
    col_ref,
    send_ref,
    out_hbm,
    part_ref,
    seed_ref,
    inv_ref,
    shapes_ref,
    w_ref,
    gain_pad,
    left_hot,
    upper_hot,
    block_a,
    block_b,
    index_rows,
    value_rows,
    m_high,
    m_low,
    t_high,
    t_low,
    mg_high,
    mg_low,
    p_ref,
    sel_ref,
    x_ref,
    z_ref,
    base_ref,
    ab_ref,
    ab_low,
    q_all,
    ghost_out,
    ghost_in,
    in_sem,
    q_send,
    q_recv,
    g_send,
    g_recv,
):
    nvar, count, owned = seed_ref.shape
    modes = shapes_ref.shape[1]
    rows = count * nvar
    halo = send_ref.shape[1]
    nfaces = faces_ref.shape[1]
    me = lax.axis_index("cell")
    lower, upper = lax.rem(me + n - 1, n), lax.rem(me + 1, n)
    peers = partners(me, n)
    loads = [
        pltpu.make_async_copy(src, dst, in_sem.at[k])
        for k, (src, dst) in enumerate(
            [(seed_hbm, seed_ref), (shapes_hbm, shapes_ref), (inv_hbm, inv_ref)]
        )
    ]
    for load in loads:
        load.start()

    barrier = pltpu.get_barrier_semaphore()
    for d in range(1, n):
        pl.semaphore_signal(barrier, inc=1, device_id={"cell": peers[d]}, device_id_type=pl.DeviceIdType.MESH)

    left = faces_ref[0:1, :].astype(jnp.int16)
    right = faces_ref[1:2, :].astype(jnp.int16)
    p_tile, q_tile = bf16_factors(g_ref[...])
    p_tile, q_tile = p_tile.astype(F32), q_tile.astype(F32)
    p_row = jnp.concatenate([p_tile[k : k + 1, :] for k in range(nfaces // 128)], axis=1).astype(BF16)
    q_row = jnp.concatenate([q_tile[k : k + 1, :] for k in range(nfaces // 128)], axis=1).astype(BF16)
    step = 128
    wide = 256
    tall = owned + halo

    for k, row in enumerate((left, right)):
        index_rows[k] = jnp.broadcast_to(row, (16, nfaces))
    for k, row in enumerate((p_row, q_row)):
        value_rows[k] = jnp.broadcast_to(row, (16, nfaces))
    sixteen = lax.broadcasted_iota(jnp.int32, (16, 128), 0)

    def hot(side, start, size):
        near = index_rows[side]
        value = value_rows[side]
        zero = jnp.zeros((16, nfaces), BF16)
        strips = []
        for k in range(size // 16):
            line = (sixteen + (start + 16 * k)).astype(jnp.int16)
            strips.append(jnp.where(near == jnp.concatenate([line] * (nfaces // 128), axis=1), value, zero))
        return jnp.concatenate(strips, axis=0)

    cut = owned // 2

    def split_block(at, block_ref, r0, r1):
        here = pl.ds(at, wide)
        block = block_ref[0 : r1 - r0, :]
        high, low = split_f8(block)
        m_high[r0:r1, here] = high
        m_low[r0:r1, here] = low
        high, low = split_f8(block.T)
        t_high[here, r0:r1] = high
        t_low[here, r0:r1] = low

    @pl.loop(0, tall // step)
    def _(t):
        at = pl.multiple_of(t * step, step)
        left_hot[pl.ds(at, step), :] = hot(0, at, step)


    send_row = jnp.concatenate([send_ref[0:1, :], send_ref[1:2, :]], axis=1)
    loads[0].wait()
    loads[1].wait()

    @pl.loop(0, owned // wide)
    def _(t):
        at = pl.multiple_of(t * wide, wide)
        here = pl.ds(at, wide)
        sel_ref[here, 0 : 2 * halo] = jnp.where(
            send_row - at == lax.broadcasted_iota(jnp.int32, (wide, 2 * halo), 0), 1.0, 0.0
        ).astype(BF16)
        pad = jnp.zeros((MODE_ROWS - modes, wide), F32)
        lines = []
        for v in range(nvar):
            lines += [shapes_ref[v, :, here], pad]
            z_ref[v * count : (v + 1) * count, here] = seed_ref[v, :, here]
            base_ref[v * count : (v + 1) * count, here] = seed_ref[v, :, here]
        lines.append(jnp.zeros((128 - nvar * MODE_ROWS, wide), F32))
        high, low = split(jnp.concatenate(lines, axis=0))
        p_ref[0:128, here] = high
        p_ref[128:256, here] = low
        sel_ref[here, 2 * halo : 2 * halo + 128] = high.astype(F32).T.astype(BF16)
        sel_ref[here, 2 * halo + 128 :] = low.astype(F32).T.astype(BF16)
        eye_line = lax.broadcasted_iota(jnp.int32, (count, rows), 0)
        eye_lane = lax.broadcasted_iota(jnp.int32, (count, rows), 1)
        eye = lax.rem(eye_lane, count) == eye_line
        blocks = []
        for side in range(2):
            for w in range(nvar):
                row = jnp.concatenate([flux_ref[v, w][side : side + 1, :] for v in range(nvar)], axis=1)
                blocks.append(jnp.where(eye, jnp.broadcast_to(row, (count, rows)), 0.0))
        line = lax.broadcasted_iota(jnp.int32, (rows, rows), 0)
        lane = lax.broadcasted_iota(jnp.int32, (rows, rows), 1)
        apart = lax.rem(lane, count) - lax.rem(line, count)
        spectral = jnp.zeros((rows, rows), F32)
        for d, weight in enumerate(spectral_weights(count), 1):
            spectral = jnp.where(apart == d, weight, jnp.where(apart == -d, -weight, spectral))
        spectral = jnp.where(lax.div(lane, count) == lax.div(line, count), spectral, 0.0)
        w_high, w_low = split(jnp.concatenate(blocks + [spectral], axis=0))
        lane = lax.broadcasted_iota(jnp.int32, (rows, 3 * rows), 1)
        line = lax.broadcasted_iota(jnp.int32, (rows, 3 * rows), 0)
        first = jnp.where((lane == line) | (lane == line + rows), 1.0, 0.0).astype(BF16)
        last = jnp.where(lane == line + 2 * rows, 1.0, 0.0).astype(BF16)
        w_ref[...] = (mm(w_high, first) + mm(w_low, last)).astype(BF16)
        right_now = hot(1, at, wide)
        earlier = lax.rem(t + owned // wide - 1, owned // wide)
        split_block(pl.multiple_of(earlier * wide, wide), block_b, 0, cut)
        block_a[...] = mm_nt(left_hot[cut:tall, :], right_now)
        split_block(at, block_a, cut, owned)
        high, low = split(block_a[owned - cut : tall - cut, :])
        mg_high[0:halo, here] = high
        mg_low[0:halo, here] = low
        block_b[...] = mm_nt(left_hot[0:cut, :], right_now)

    split_block(owned - wide, block_b, 0, cut)

    def build_ghost_matrix():
        upper_hot[...] = hot(1, owned + halo, halo)

        @pl.loop(0, owned // wide)
        def _(t):
            at = pl.multiple_of(t * wide, wide)
            high, low = split(mm_nt(upper_hot[...], left_hot[pl.ds(at, wide), :]))
            mg_high[halo:, pl.ds(at, wide)] = high
            mg_low[halo:, pl.ds(at, wide)] = low

    loads[2].wait()
    gain_pad[...] = jnp.zeros((1, 128), F32)
    gain_pad[:, 0:modes] = gain_ref[...]
    colours = col_ref[...]

    def update(colour):
        mask = colours == colour
        for w in range(nvar):
            spot = slice(w * count, (w + 1) * count)
            total = inv_ref[0, w].astype(F32) * z_ref[0:count, :]
            for v in range(1, nvar):
                total = total + inv_ref[v, w].astype(F32) * z_ref[v * count : (v + 1) * count, :]
            x_ref[spot, :] = jnp.where(mask, total, x_ref[spot, :])

    def coupling():
        value = x_ref[...]
        top = jnp.max(jnp.abs(value), axis=0, keepdims=True)
        top = jnp.maximum(jnp.max(top, axis=1, keepdims=True), 1e-30)
        scale = SPAN / top
        high, low = split(value)
        both = mm(w_ref[...], jnp.concatenate([high, low, high], axis=0))
        for side in range(2):
            part = both[side * rows : (side + 1) * rows]
            high, low = split(part)
            ab_ref[side, 0:rows, :] = high
            ab_ref[side, rows:, :] = low
            rough = jnp.concatenate([part * scale, jnp.zeros((96 - rows, owned), F32)], axis=0)
            ab_low[side] = rough.astype(F8)
        one = mm(ab_ref[0], m_high[...]) + mm(ab_ref[1], t_high[...])
        two = mm(ab_low[0], m_low[...]) + mm(ab_low[1], t_low[...])
        z_ref[...] = both[2 * rows :] + (one[:rows] + one[rows:] + two[:rows] * (top * (1.0 / (SPAN * LIFT))))

    def modal_copies(turn):
        return [
            pltpu.make_async_remote_copy(
                src_ref=q_all.at[turn, me],
                dst_ref=q_all.at[turn, me],
                send_sem=q_send.at[turn],
                recv_sem=q_recv.at[turn],
                device_id={"cell": peers[d]},
                device_id_type=pl.DeviceIdType.MESH,
            )
            for d in range(n - 1, 0, -1)
        ]

    def wait_modal(turn):
        every = q_all.at[turn, pl.ds(0, n - 1)]
        pltpu.make_async_copy(every, every, q_recv.at[turn]).wait()

    def ghost_copies(turn):
        return [
            pltpu.make_async_remote_copy(
                src_ref=ghost_out.at[turn, way],
                dst_ref=ghost_in.at[turn, 1 - way],
                send_sem=g_send.at[turn, way],
                recv_sem=g_recv.at[turn, way],
                device_id={"cell": lower if way == 0 else upper},
                device_id_type=pl.DeviceIdType.MESH,
            )
            for way in range(2)
        ]

    def start_exchange(turn):
        high, low = split(x_ref[...])
        every = mm(jnp.concatenate([high, low], axis=0), sel_ref[...])
        every = every[:rows] + every[rows:]
        @pl.when(turn == 0)
        def _():
            pl.semaphore_wait(barrier, n - 1)

        @pl.when(turn < ITERS - 1)
        def _():
            ghost_out[turn, 0] = every[:, :halo]
            ghost_out[turn, 1] = every[:, halo : 2 * halo]
            for copy in ghost_copies(turn):
                copy.start()

        gram = every[:, 2 * halo : 2 * halo + 128] + every[:, 2 * halo + 128 :]
        part = gram[0:count, 0:MODE_ROWS]
        for v in range(1, nvar):
            part = part + gram[v * count : (v + 1) * count, v * MODE_ROWS : (v + 1) * MODE_ROWS]
        size = count // 4
        pieces = [part[k * size : (k + 1) * size] for k in range(4)]
        q_all[turn, me] = jnp.concatenate(pieces + [jnp.zeros((size, 128 - 4 * MODE_ROWS), F32)], axis=1)
        for copy in modal_copies(turn):
            copy.start()

    def modal_sum(turn):
        total = q_all[turn, 0]
        for d in range(1, n):
            total = total + q_all[turn, d]
        return jnp.concatenate([total[:, k * MODE_ROWS : (k + 1) * MODE_ROWS] for k in range(4)], axis=0)

    x_ref[...] = jnp.zeros((rows, owned), F32)
    @pl.loop(0, ITERS)
    def _(sweep):
        @pl.when(sweep > 0)
        def _():
            coupling()

            @pl.when(sweep == 1)
            def _():
                build_ghost_matrix()

            for copy in ghost_copies(sweep - 1):
                copy.wait_recv()
            wait_modal(sweep - 1)
            low_part = ghost_in[sweep - 1, 0]
            up_part = ghost_in[sweep - 1, 1]
            high, low = split(jnp.concatenate([low_part, up_part], axis=1))
            both = mm(w_ref[0 : 2 * rows, :], jnp.concatenate([high, low, high], axis=0))
            ghost_ab = jnp.concatenate([both[:rows, :halo], both[rows:, halo:]], axis=1)
            ghost_high, ghost_low = split(ghost_ab)
            lam = modal_sum(sweep - 1) * gain_pad[:, :MODE_ROWS]
            lam = jnp.concatenate([lam] * nvar + [jnp.zeros((count, 128 - nvar * MODE_ROWS), F32)], axis=1)
            lam = jnp.concatenate([lam] * nvar, axis=0)
            lane = lax.broadcasted_iota(jnp.int32, (rows, 128), 1)
            line = lax.broadcasted_iota(jnp.int32, (rows, 128), 0)
            lam = jnp.where(lax.div(lane, MODE_ROWS) == lax.div(line, count), -lam, 0.0)
            lam_high, lam_low = split(lam)
            term = mm(jnp.concatenate([ghost_high, ghost_low], axis=0), mg_high[...]) + mm(
                jnp.concatenate([lam_high, lam_low], axis=0), p_ref[0:128, :]
            )
            rest = mm(ghost_high, mg_low[...]) + mm(lam_high, p_ref[128:256, :])
            term = term[:rows] + term[rows:] + rest
            for v in range(nvar):
                spot = slice(v * count, (v + 1) * count)
                base = seed_ref[v] - term[spot]
                base_ref[spot, :] = base
                z_ref[spot, :] = base - z_ref[spot, :]
            update(0)

        @pl.when(sweep == 0)
        def _():
            update(0)

        coupling()
        z_ref[...] = base_ref[...] - z_ref[...]
        update(1)
        start_exchange(sweep)

    out_hbm[...] = x_ref[...]
    for turn in range(ITERS):
        every = q_all.at[turn, pl.ds(0, n - 1)]
        pltpu.make_async_copy(every, every, q_send.at[turn]).wait()
        if turn < ITERS - 1:
            for copy in ghost_copies(turn):
                copy.wait_send()
    wait_modal(ITERS - 1)
    part_ref[...] = modal_sum(ITERS - 1)[:, :modes]


def partners(me, n):
    if n & (n - 1):
        return [lax.rem(me + d, n) for d in range(n)]
    places = []
    for d in range(n):
        place = me
        bit = 1
        while bit < n:
            if d & bit:
                place = place + bit - 2 * bit * lax.rem(lax.div(me, bit), 2)
            bit *= 2
        places.append(place)
    return places


def hand_over(out_ref, part_ref, out_final, part_final, sem):
    first = pltpu.make_async_copy(out_ref, out_final, sem.at[0])
    second = pltpu.make_async_copy(part_ref, part_final, sem.at[1])
    first.start()
    second.start()
    first.wait()
    second.wait()


def local(
    adjoint_seed,
    inv_blocks,
    flux_jacobians,
    modal_shapes,
    modal_gain,
    face_cells,
    face_weights,
    colours,
    send_cells,
):
    n = lax.axis_size("cell")
    count, nvar, owned = adjoint_seed.shape
    modes = modal_shapes.shape[0]
    rows = count * nvar
    halo = send_cells.shape[1]
    nfaces = face_weights.shape[0]
    inverse = jnp.transpose(inv_blocks, (1, 2, 0, 3))
    vmem = pl.BlockSpec(memory_space=pltpu.VMEM)
    hbm = pl.BlockSpec(memory_space=pl.ANY)
    tall = owned + halo
    turns = ITERS
    out, part = pl.pallas_call(
        functools.partial(kernel, n),
        out_shape=(
            pltpu.VMEM((rows, owned), F32),
            pltpu.VMEM((count, modes), F32),
        ),
        in_specs=[hbm, hbm, vmem, hbm] + [vmem] * 5,
        out_specs=(vmem, vmem),
        scratch_shapes=[
            pltpu.VMEM((nvar, count, owned), F32),
            pltpu.VMEM((nvar, nvar, count, owned), BF16),
            pltpu.VMEM((nvar, modes, owned), F32),
            pltpu.VMEM((3 * rows, 3 * rows), BF16),
            pltpu.VMEM((1, 128), F32),
            pltpu.VMEM((tall, nfaces), BF16),
            pltpu.VMEM((halo, nfaces), BF16),
            pltpu.VMEM((owned // 2 + halo, 256), F32),
            pltpu.VMEM((owned // 2, 256), F32),
            pltpu.VMEM((2, 16, nfaces), jnp.int16),
            pltpu.VMEM((2, 16, nfaces), BF16),
            pltpu.VMEM((owned, owned), BF16),
            pltpu.VMEM((owned, owned), F8),
            pltpu.VMEM((owned, owned), BF16),
            pltpu.VMEM((owned, owned), F8),
            pltpu.VMEM((2 * halo, owned), BF16),
            pltpu.VMEM((2 * halo, owned), BF16),
            pltpu.VMEM((256, owned), BF16),
            pltpu.VMEM((owned, 2 * halo + 256), BF16),
            pltpu.VMEM((rows, owned), F32),
            pltpu.VMEM((rows, owned), F32),
            pltpu.VMEM((rows, owned), F32),
            pltpu.VMEM((2, 2 * rows, owned), BF16),
            pltpu.VMEM((2, 96, owned), F8),
            pltpu.VMEM((turns, n, count // 4, 128), F32),
            pltpu.VMEM((turns - 1, 2, rows, halo), F32),
            pltpu.VMEM((turns - 1, 2, rows, halo), F32),
            pltpu.SemaphoreType.DMA((3,)),
            pltpu.SemaphoreType.DMA((turns,)),
            pltpu.SemaphoreType.DMA((turns,)),
            pltpu.SemaphoreType.DMA((turns - 1, 2)),
            pltpu.SemaphoreType.DMA((turns - 1, 2)),
        ],
        compiler_params=pltpu.CompilerParams(
            collective_id=0, has_side_effects=True, vmem_limit_bytes=56 * 1024 * 1024
        ),
    )(
        jnp.transpose(adjoint_seed, (1, 0, 2)),
        inverse,
        jnp.transpose(flux_jacobians, (2, 3, 0, 1)),
        jnp.transpose(modal_shapes, (1, 0, 2)),
        modal_gain[None, :],
        face_cells,
        face_weights.reshape(nfaces // 128, 128),
        colours[None, :],
        send_cells,
    )
    out, part = pl.pallas_call(
        hand_over,
        out_shape=(
            jax.ShapeDtypeStruct((rows, owned), F32),
            jax.ShapeDtypeStruct((count, modes), F32),
        ),
        in_specs=[vmem, vmem],
        out_specs=(hbm, hbm),
        scratch_shapes=[
            pltpu.SemaphoreType.DMA((2,)),
        ],
    )(
        pltpu.with_memory_space_constraint(out, pltpu.VMEM),
        pltpu.with_memory_space_constraint(part, pltpu.VMEM),
    )
    return jnp.transpose(out.reshape(nvar, count, owned), (1, 0, 2)), part


def solution(mesh):
    return jax.shard_map(
        local,
        mesh=mesh,
        in_specs=(
            P("group", None, "cell"),
            P("group", None, None, "cell"),
            P(None, "group", None, None),
            P(None, None, "cell"),
            P("group"),
            P(None, "cell"),
            P("cell"),
            P("cell"),
            P(None, "cell"),
        ),
        out_specs=(P("group", None, "cell"), P("group", None)),
        check_vma=False,
    )
```
